1024 devices in a mesh: clip: 16 (over y, x), tm: 64 (over z, core).
Axes of the slice: x: 4, y: 4, z: 32, core: 2. Of those that a mesh axis runs over, the one named last changes fastest.
Arguments:
- embeddings: bfloat16 [256, 256, 768], P('clip', 'tm'), may hold values from -6 to 6
- lengths: int32 [256], replicated, may hold values from 64 to 256, as said below
- pairs: int32 [2048, 2], replicated, may hold values from 0 to 255, as said below
- scaled_weight: float32 [2048], P(('clip', 'tm')), may hold values from 64 to 1024
Outputs:
- pair_loss: float32 [2048], P(('clip', 'tm'))
- grad_embeddings: bfloat16 [256, 256, 768], P('clip', 'tm')
The draws below stay inside these ranges and needn't reach their ends.
Inputs may be any that keep to these rules, and one draw needn't show every extreme that they name: `lengths`: each clip's length in frames; some clip has exactly 256. `pairs`: clip ids. The first clip of row r lies in owner shard r // 128, i.e. among ids of that shard's 16 clips; the partner differs from the first clip. The rows of one owner shard name at most 4 distinct partner clips of any one shard, and exactly 4 of some shard.
All inputs are finite; a program needn't handle non-finite values.
Results may differ from the reference program's by a relative error of at most 0.025.
Values may be sent and summed in bfloat16 or wider, within the bound.
No kernel may reach another device: no remote copies, remote signals or barrier semaphores. Data moves between devices by JAX's collectives and lax.ppermute only.
A program may use at most 32 MiB of HBM per device.

```python
import math
import jax
import jax.numpy as jnp
from jax import lax

D = 768
FRAMES = 256
CLIP_DEV = 16
PAIR_OWN = 128
PAIRS = 2048
CLIPS = 256
N_CLIP = 16


def draw_lengths(key, part):
    key = jax.random.fold_in(key, 29)
    keys = jax.random.split(key, 2)
    drawn = jax.random.randint(keys[0], (CLIPS,), FRAMES // 4, FRAMES + 1)
    longest = jax.random.randint(keys[1], (), 0, CLIPS)
    return jnp.where(jnp.arange(CLIPS) == longest, FRAMES, drawn).astype(jnp.int32)


def draw_pairs(key, part):
    key = jax.random.fold_in(key, 17)
    keys = jax.random.split(key, 6)
    capacity = min(CLIP_DEV // 4, PAIR_OWN // 4)
    rows = jnp.arange(PAIR_OWN, dtype=jnp.int32)
    owners = jnp.arange(N_CLIP, dtype=jnp.int32)
    hot_source = jax.random.randint(keys[0], (N_CLIP,), 0, N_CLIP)
    window = jax.random.randint(keys[1], (N_CLIP, N_CLIP), 0, CLIP_DEV)
    other_source = jax.random.randint(keys[2], (N_CLIP, PAIR_OWN), 0, N_CLIP)
    heavy = rows[None, :] < 2 * capacity
    source = jnp.where(heavy, hot_source[:, None], other_source)
    inner = jnp.where(heavy, rows[None, :] % capacity, jax.random.randint(keys[3], (N_CLIP, PAIR_OWN), 0, capacity))
    start = jnp.take_along_axis(window, source, axis=1)
    partner_slot = (start + inner) % CLIP_DEV
    first_slot = jax.random.randint(keys[4], (N_CLIP, PAIR_OWN), 0, CLIP_DEV)
    clash = (source == owners[:, None]) & (first_slot == partner_slot)
    first_slot = jnp.where(clash, (first_slot + CLIP_DEV // 2) % CLIP_DEV, first_slot)
    scores = jax.random.randint(keys[5], (N_CLIP, PAIR_OWN), 0, 1 << 20) * PAIR_OWN + rows[None, :]
    order = jnp.argsort(scores, axis=1)
    first = owners[:, None] * CLIP_DEV + jnp.take_along_axis(first_slot, order, axis=1)
    partner = jnp.take_along_axis(source * CLIP_DEV + partner_slot, order, axis=1)
    return jnp.stack([first, partner], axis=-1).reshape(PAIRS, 2).astype(jnp.int32)


def shard_levels(key, dims, shards, least, top_value):
    def one(axis_at, parts):
        steps = jax.random.uniform(jax.random.fold_in(jax.random.fold_in(key, 6), axis_at), (parts,), jnp.float32, least / len(shards), top_value / len(shards))
        return jnp.repeat(jnp.exp(steps), dims[axis_at] // parts).reshape((-1,) + (1,) * (len(dims) - axis_at - 1))

    factor_of = one(*shards[0])
    for cut in shards[1:]:
        factor_of = factor_of * one(*cut)
    return factor_of


def noise(own_key, extent, deviation, reach, shards=(), kind=jnp.bfloat16):
    array = deviation * jax.random.normal(own_key, extent, jnp.float32)
    if shards:
        array = array * shard_levels(own_key, extent, shards, -0.22, 0.18)
    return jnp.clip(array, -reach, reach).astype(kind)


def setup_inputs(seed: int = 0) -> dict:
    key_list = jax.random.split(jax.random.key(seed), 5)
    return {
        "embeddings": noise(key_list[0], (CLIPS, FRAMES, D), 1.0, 6.0, ((0, 16), (1, 64))),
        "lengths": draw_lengths(jax.random.fold_in(key_list[4], 71), 0),
        "pairs": draw_pairs(jax.random.fold_in(key_list[4], 71), 0),
        "scaled_weight": jnp.clip(jnp.exp(math.log(1024.0) - 2.7725887 * jax.random.uniform(key_list[3], (PAIRS,), jnp.float32) ** shard_levels(key_list[3], (PAIRS,), ((0, 1024),), -0.2, 0.2)), 64.0, 1024.0),
    }


score_scale = 2.0
spread_floor = 1.0
log_weight = 0.1
epsilon = 1e-06

def normalize(values):
    as_float = values.astype(jnp.float32)
    scaled = as_float * lax.rsqrt(lax.optimization_barrier(jnp.mean(as_float * as_float, axis=-1, keepdims=True)) + epsilon)
    return scaled.astype(jnp.bfloat16)

def cross_scores(left, right, factor):
    products = lax.dot_general(left, right, (((1,), (1,)), ((), ())), preferred_element_type=jnp.float32)
    return products * factor

def pair_value(first_clip, partner_clip, len_first, len_partner):
    frames = first_clip.shape[0]
    feature = first_clip.shape[1]
    factor = score_scale / math.sqrt(feature)
    n_first = normalize(first_clip)
    n_partner = normalize(partner_clip)
    positions = jnp.arange(frames, dtype=jnp.int32)
    forward_scores = cross_scores(n_first, n_partner, factor)
    forward_exp = jnp.where((positions < len_partner)[None, :], jnp.exp(forward_scores), 0.0)
    forward_prob = (forward_exp / lax.optimization_barrier(jnp.sum(forward_exp, axis=1, keepdims=True))).astype(jnp.bfloat16)
    soft_match = jnp.dot(forward_prob, n_partner, preferred_element_type=jnp.float32).astype(jnp.bfloat16)
    backward_scores = cross_scores(soft_match, n_first, factor)
    backward_exp = jnp.where((positions < len_first)[None, :], jnp.exp(backward_scores), 0.0)
    back_prob = backward_exp / lax.optimization_barrier(jnp.sum(backward_exp, axis=1, keepdims=True))
    frame_time = positions.astype(jnp.float32)
    mean_time = lax.optimization_barrier(jnp.sum(back_prob * frame_time[None, :], axis=1))
    offsets = frame_time[None, :] - mean_time[:, None]
    spread = lax.optimization_barrier(jnp.sum(back_prob * offsets * offsets, axis=1)) + spread_floor
    missed = frame_time - mean_time
    frame_terms = missed * missed / spread + log_weight * jnp.log(spread)
    valid_rows = positions < len_first
    return jnp.sum(jnp.where(valid_rows, frame_terms, 0.0)) / len_first.astype(jnp.float32)

def pair_grads(first_clip, partner_clip, len_first, len_partner, weight):
    value, pullback = jax.vjp(lambda left, right: pair_value(left, right, len_first, len_partner), first_clip, partner_clip)
    grad_first, grad_partner = pullback(weight)
    return (value, grad_first.astype(jnp.bfloat16), grad_partner.astype(jnp.bfloat16))

def reference(embeddings, lengths, pairs, scaled_weight):
    clips, frames, feature = embeddings.shape
    grouped = pairs.reshape(N_CLIP, PAIR_OWN, 2)
    weights = scaled_weight.reshape(N_CLIP, PAIR_OWN)

    def one_pair(pair_item):
        pair_ids, weight = pair_item
        return pair_grads(embeddings[pair_ids[0]], embeddings[pair_ids[1]], lengths[pair_ids[0]], lengths[pair_ids[1]], weight)

    def owner_step(grad_total, owner_item):
        pair_ids, weight = owner_item
        losses, grad_first, grad_partner = lax.map(one_pair, (pair_ids, weight))
        grad_total = grad_total.at[pair_ids[:, 0]].add(grad_first.astype(jnp.float32))
        partner_sum = jnp.zeros((clips, frames, feature), jnp.float32).at[pair_ids[:, 1]].add(grad_partner.astype(jnp.float32))
        partner_sum = lax.optimization_barrier(partner_sum.astype(jnp.bfloat16))
        grad_total = grad_total + partner_sum.astype(jnp.float32)
        return (grad_total, losses)
    grad_total, losses = lax.scan(owner_step, jnp.zeros((clips, frames, feature), jnp.float32), (grouped, weights))
    return (losses.reshape(-1), grad_total.astype(jnp.bfloat16))
```

```python
import math

import jax
import jax.numpy as jnp
from jax import lax
from jax.sharding import PartitionSpec as P

score_scale = 2.0
spread_floor = 1.0
log_weight = 0.1
epsilon = 1e-06
slots = 4


def dot(left, right, contract, out=jnp.float32):
    return lax.dot_general(left, right, (contract, ((), ())), preferred_element_type=out)


def split(values, parts):
    pieces = []
    for _ in range(parts):
        piece = lax.reduce_precision(values, 8, 7)
        pieces.append(piece.astype(jnp.bfloat16))
        values = values - piece
    return pieces


def with_scalars(rows, scalars):
    pieces = jnp.stack(split(scalars, 3))
    pad = ((0, 8 - pieces.shape[0]), (0, rows.shape[1] - pieces.shape[1]))
    return jnp.concatenate([rows, jnp.pad(pieces, pad)], axis=0)


def without_scalars(packed, count):
    pieces = packed[-8:-5, :count].astype(jnp.float32)
    return packed[:-8], (pieces[0] + pieces[1]) + pieces[2]


def pair_grads(n_first, n_partner, len_first, len_partner, weight):
    frames, feature = n_first.shape
    factor = score_scale / math.sqrt(feature)
    columns = lax.broadcasted_iota(jnp.int32, (frames, frames), 1)
    column_time = columns.astype(jnp.float32)
    scores = dot(n_first, n_partner, ((1,), (1,))) * factor
    forward_exp = jnp.where(columns < len_partner, jnp.exp(scores), 0.0)
    forward_prob = forward_exp / jnp.sum(forward_exp, axis=1, keepdims=True)
    prob = forward_prob.astype(jnp.bfloat16)
    high, low = split(scores, 2)
    backward_scores = dot(prob, high, ((1,), (1,))) + dot(prob, low, ((1,), (1,)))
    backward_exp = jnp.where(columns < len_first, jnp.exp(backward_scores), 0.0)
    back_prob = backward_exp / jnp.sum(backward_exp, axis=1, keepdims=True)
    mean_time = jnp.sum(back_prob * column_time, axis=1, keepdims=True)
    offsets = column_time - mean_time
    squares = offsets * offsets
    variance = jnp.sum(back_prob * squares, axis=1, keepdims=True)
    spread = variance + spread_floor
    rows = lax.broadcasted_iota(jnp.int32, (frames, 1), 0)
    missed = rows.astype(jnp.float32) - mean_time
    ratio = missed / spread
    terms = missed * ratio + log_weight * jnp.log(spread)
    valid = rows < len_first
    length = len_first.astype(jnp.float32)
    loss = jnp.sum(jnp.where(valid, terms, 0.0)) / length
    row_weight = jnp.where(valid, weight / length, 0.0)
    d_mean = -2.0 * ratio * row_weight
    d_spread = (log_weight / spread - ratio * ratio) * row_weight
    d_back = back_prob * (d_mean * offsets + d_spread * (squares - variance))
    d_back = d_back.astype(jnp.bfloat16)
    d_prob = dot(d_back, high, ((1,), (0,))) + dot(d_back, low, ((1,), (0,)))
    d_scores = forward_prob * (d_prob - jnp.sum(forward_prob * d_prob, axis=1, keepdims=True))
    d_scores = d_scores + dot(d_back, prob, ((0,), (0,)))
    d_scores = (d_scores * factor).astype(jnp.bfloat16)
    grad_first = dot(d_scores, n_partner, ((1,), (0,))).astype(jnp.bfloat16)
    grad_partner = dot(d_scores, n_first, ((0,), (0,))).astype(jnp.bfloat16)
    return loss, grad_first, grad_partner


def shards(embeddings, lengths, pairs, scaled_weight):
    owners = lax.axis_size("clip")
    times = lax.axis_size("tm")
    clip_count, block, feature = embeddings.shape
    per_device = scaled_weight.shape[0]
    per_owner = per_device * times
    row_width = block * feature
    spots = times // owners
    column = lax.axis_index("clip")
    time_index = lax.axis_index("tm")
    owner = time_index // spots
    spot = time_index % spots
    turn = (column - owner + owners) % owners
    place = turn * spots + spot

    long_range = [[a + spots * i for i in range(owners)] for a in range(spots)]
    home = [
        [((m + c) % owners) * times + spots * c + q for m in range(owners) for q in range(spots)]
        for c in range(owners)
    ]
    plane = [
        [((m + t // spots) % owners) * times + t for m in range(owners)] for t in range(times)
    ]
    swap = [
        (c * times + t, ((t // spots + c) % owners) * times + c * spots + t % spots)
        for c in range(owners)
        for t in range(times)
    ]
    back = [(there, here) for here, there in swap]
    both = ("clip", "tm")

    as_float = embeddings.astype(jnp.float32)
    scale = lax.rsqrt(jnp.mean(as_float * as_float, axis=-1, keepdims=True) + epsilon)
    normalized = (as_float * scale).astype(jnp.bfloat16)

    packed = with_scalars(normalized.reshape(clip_count * block, feature), scaled_weight)

    grouped = pairs.reshape(owners, per_owner, 2)
    clips = jnp.arange(owners * clip_count, dtype=jnp.int32)
    used = jnp.any(grouped[:, :, 1, None] == clips[None, None, :], axis=1)
    before = (clips[:, None] // clip_count == clips[None, :] // clip_count) & (
        clips[:, None] < clips[None, :]
    )
    rank = dot(used.astype(jnp.bfloat16), before.astype(jnp.bfloat16), ((1,), (0,)))
    rank = jnp.where(used, rank.astype(jnp.int32), -1)
    mine = lax.dynamic_slice_in_dim(rank, column * clip_count, clip_count, 1)
    slot_ids = jnp.arange(slots, dtype=jnp.int32)
    chosen = mine[:, None, :] == slot_ids[None, :, None]
    chosen = chosen.reshape(owners * slots, clip_count).astype(jnp.bfloat16)

    outgoing = dot(
        chosen, normalized.reshape(clip_count, row_width), ((1,), (0,)), jnp.bfloat16
    ).reshape(owners, slots * block, feature)
    outgoing = lax.all_to_all(
        outgoing, "tm", 0, 0, axis_index_groups=long_range, tiled=True
    )
    outgoing, packed = lax.optimization_barrier((outgoing, packed))
    firsts, weight = without_scalars(lax.ppermute(packed, both, swap), per_device)
    partners = lax.all_to_all(outgoing, both, 0, 0, axis_index_groups=plane, tiled=True)

    owned = lax.dynamic_index_in_dim(grouped, owner, 0, keepdims=False)
    owned_rank = lax.dynamic_index_in_dim(rank, owner, 0, keepdims=False)
    first_hot = (
        (owned[:, 0] - owner * clip_count)[:, None]
        == jnp.arange(clip_count, dtype=jnp.int32)[None, :]
    ).astype(jnp.bfloat16)
    partner_is = owned[:, 1][:, None] == clips[None, :]
    partner_slot = jnp.sum(jnp.where(partner_is, owned_rank[None, :], 0), axis=1)
    source = (owned[:, 1] // clip_count - owner + owners) % owners
    partner_slot = partner_slot + source * slots
    partner_hot = (
        partner_slot[:, None] == jnp.arange(owners * slots, dtype=jnp.int32)[None, :]
    ).astype(jnp.bfloat16)

    first_rows = dot(
        first_hot, firsts.reshape(clip_count, row_width), ((1,), (0,)), jnp.bfloat16
    ).reshape(times, per_device, block, feature)
    partner_rows = dot(
        partner_hot, partners.reshape(owners * slots, row_width), ((1,), (0,)), jnp.bfloat16
    ).reshape(times, per_device, block, feature)
    rows = jnp.concatenate([first_rows, partner_rows], axis=1)
    rows = rows.reshape(times, 2 * per_device * block, feature)
    frames = lax.all_to_all(rows, both, 0, 0, axis_index_groups=home, tiled=True)
    frames = frames.reshape(times, 2, per_device, block, feature).transpose(1, 2, 0, 3, 4)
    frames = frames.reshape(2, per_device, times * block, feature)

    my_ids = lax.dynamic_slice_in_dim(owned, place * per_device, per_device, 0)
    len_first = jnp.take(lengths, my_ids[:, 0])
    len_partner = jnp.take(lengths, my_ids[:, 1])
    losses, grad_first, grad_partner = jax.vmap(pair_grads)(
        frames[0], frames[1], len_first, len_partner, weight
    )

    grads = jnp.stack([grad_first, grad_partner]).reshape(
        2, per_device, times, block, feature
    )
    grads = grads.transpose(2, 0, 1, 3, 4).reshape(times, 2 * per_device * block, feature)
    returned = lax.all_to_all(grads, both, 0, 0, axis_index_groups=home, tiled=True)
    returned = returned.reshape(times, 2, per_device, row_width)
    first_back = returned[:, 0].reshape(per_owner, row_width)
    partner_back = returned[:, 1].reshape(per_owner, row_width)
    first_sum = dot(first_hot, first_back, ((0,), (0,))).astype(jnp.bfloat16)
    first_sum = with_scalars(first_sum.reshape(clip_count * block, feature), losses)
    first_sum = lax.ppermute(first_sum, both, back)
    partner_sum = dot(partner_hot, partner_back, ((0,), (0,))).astype(jnp.bfloat16)
    partner_sum = partner_sum.reshape(owners, slots * block, feature)
    partner_sum = lax.all_to_all(partner_sum, both, 0, 0, axis_index_groups=plane, tiled=True)
    partner_sum, first_sum = lax.optimization_barrier((partner_sum, first_sum))
    first_sum, losses = without_scalars(first_sum, per_device)
    partner_sum = lax.all_to_all(
        partner_sum, "tm", 0, 0, axis_index_groups=long_range, tiled=True
    )
    total = dot(chosen, partner_sum.reshape(owners * slots, row_width), ((0,), (0,)))
    total = total.reshape(clip_count, block, feature)
    total = total + first_sum.reshape(clip_count, block, feature).astype(jnp.float32)
    unit = as_float * scale
    gradient = scale * (total - unit * jnp.mean(total * unit, axis=-1, keepdims=True))
    return (losses, gradient.astype(jnp.bfloat16))


def solution(mesh):
    in_specs = (P("clip", "tm", None), P(), P(), P(("clip", "tm")))
    out_specs = (P(("clip", "tm")), P("clip", "tm", None))
    return jax.shard_map(shards, mesh=mesh, in_specs=in_specs, out_specs=out_specs, check_vma=False)
```

```python
import math

import jax
import jax.numpy as jnp
from jax import lax
from jax.sharding import PartitionSpec as P

score_scale = 2.0
spread_floor = 1.0
log_weight = 0.1
epsilon = 1e-06
slots = 4


def dot(left, right, contract, out=jnp.float32):
    return lax.dot_general(left, right, (contract, ((), ())), preferred_element_type=out)


def split(values, parts):
    pieces = []
    for _ in range(parts):
        piece = lax.reduce_precision(values, 8, 7)
        pieces.append(piece.astype(jnp.bfloat16))
        values = values - piece
    return pieces


def with_scalars(rows, scalars):
    pieces = jnp.stack(split(scalars, 3))
    pad = ((0, 8 - pieces.shape[0]), (0, rows.shape[1] - pieces.shape[1]))
    return jnp.concatenate([rows, jnp.pad(pieces, pad)], axis=0)


def without_scalars(packed, count):
    pieces = packed[-8:-5, :count].astype(jnp.float32)
    return packed[:-8], (pieces[0] + pieces[1]) + pieces[2]


def pair_grads(n_first, n_partner, len_first, len_partner, weight):
    frames, feature = n_first.shape
    factor = score_scale / math.sqrt(feature)
    columns = lax.broadcasted_iota(jnp.int32, (frames, frames), 1)
    column_time = columns.astype(jnp.float32)
    scores = dot(n_first, n_partner, ((1,), (1,))) * factor
    forward_exp = jnp.where(columns < len_partner, jnp.exp(scores), 0.0)
    forward_prob = forward_exp / jnp.sum(forward_exp, axis=1, keepdims=True)
    prob = forward_prob.astype(jnp.bfloat16)
    high, low = split(scores, 2)
    backward_scores = dot(prob, high, ((1,), (1,))) + dot(prob, low, ((1,), (1,)))
    backward_exp = jnp.where(columns < len_first, jnp.exp(backward_scores), 0.0)
    back_prob = backward_exp / jnp.sum(backward_exp, axis=1, keepdims=True)
    mean_time = jnp.sum(back_prob * column_time, axis=1, keepdims=True)
    offsets = column_time - mean_time
    squares = offsets * offsets
    variance = jnp.sum(back_prob * squares, axis=1, keepdims=True)
    spread = variance + spread_floor
    rows = lax.broadcasted_iota(jnp.int32, (frames, 1), 0)
    missed = rows.astype(jnp.float32) - mean_time
    ratio = missed / spread
    terms = missed * ratio + log_weight * jnp.log(spread)
    valid = rows < len_first
    length = len_first.astype(jnp.float32)
    loss = jnp.sum(jnp.where(valid, terms, 0.0)) / length
    row_weight = jnp.where(valid, weight / length, 0.0)
    d_mean = -2.0 * ratio * row_weight
    d_spread = (log_weight / spread - ratio * ratio) * row_weight
    d_back = back_prob * (d_mean * offsets + d_spread * (squares - variance))
    d_back = d_back.astype(jnp.bfloat16)
    d_prob = dot(d_back, high, ((1,), (0,))) + dot(d_back, low, ((1,), (0,)))
    d_scores = forward_prob * (d_prob - jnp.sum(forward_prob * d_prob, axis=1, keepdims=True))
    d_scores = d_scores + dot(d_back, prob, ((0,), (0,)))
    d_scores = (d_scores * factor).astype(jnp.bfloat16)
    grad_first = dot(d_scores, n_partner, ((1,), (0,))).astype(jnp.bfloat16)
    grad_partner = dot(d_scores, n_first, ((0,), (0,))).astype(jnp.bfloat16)
    return loss, grad_first, grad_partner


def shards(embeddings, lengths, pairs, scaled_weight):
    owners = lax.axis_size("clip")
    times = lax.axis_size("tm")
    clip_count, block, feature = embeddings.shape
    per_device = scaled_weight.shape[0]
    per_owner = per_device * times
    row_width = block * feature
    spots = times // owners
    column = lax.axis_index("clip")
    time_index = lax.axis_index("tm")
    owner = time_index // spots
    spot = time_index % spots
    turn = (column - owner + owners) % owners
    place = turn * spots + spot

    long_range = [[a + spots * i for i in range(owners)] for a in range(spots)]
    home = [
        [((m + c) % owners) * times + spots * c + q for m in range(owners) for q in range(spots)]
        for c in range(owners)
    ]
    plane = [
        [((m + t // spots) % owners) * times + t for m in range(owners)] for t in range(times)
    ]
    swap = [
        (c * times + t, ((t // spots + c) % owners) * times + c * spots + t % spots)
        for c in range(owners)
        for t in range(times)
    ]
    back = [(there, here) for here, there in swap]
    both = ("clip", "tm")

    as_float = embeddings.astype(jnp.float32)
    scale = lax.rsqrt(jnp.mean(as_float * as_float, axis=-1, keepdims=True) + epsilon)
    normalized = (as_float * scale).astype(jnp.bfloat16)

    packed = with_scalars(normalized.reshape(clip_count * block, feature), scaled_weight)

    grouped = pairs.reshape(owners, per_owner, 2)
    clips = jnp.arange(owners * clip_count, dtype=jnp.int32)
    used = jnp.any(grouped[:, :, 1, None] == clips[None, None, :], axis=1)
    before = (clips[:, None] // clip_count == clips[None, :] // clip_count) & (
        clips[:, None] < clips[None, :]
    )
    rank = dot(used.astype(jnp.bfloat16), before.astype(jnp.bfloat16), ((1,), (0,)))
    rank = jnp.where(used, rank.astype(jnp.int32), -1)
    mine = lax.dynamic_slice_in_dim(rank, column * clip_count, clip_count, 1)
    slot_ids = jnp.arange(slots, dtype=jnp.int32)
    chosen = mine[:, None, :] == slot_ids[None, :, None]
    chosen = chosen.reshape(owners * slots, clip_count).astype(jnp.bfloat16)

    outgoing = dot(
        chosen, normalized.reshape(clip_count, row_width), ((1,), (0,)), jnp.bfloat16
    ).reshape(owners, slots * block, feature)
    outgoing = lax.all_to_all(
        outgoing, "tm", 0, 0, axis_index_groups=long_range, tiled=True
    )
    firsts, weight = without_scalars(lax.ppermute(packed, both, swap), per_device)
    partners = lax.all_to_all(outgoing, both, 0, 0, axis_index_groups=plane, tiled=True)

    owned = lax.dynamic_index_in_dim(grouped, owner, 0, keepdims=False)
    owned_rank = lax.dynamic_index_in_dim(rank, owner, 0, keepdims=False)
    first_hot = (
        (owned[:, 0] - owner * clip_count)[:, None]
        == jnp.arange(clip_count, dtype=jnp.int32)[None, :]
    ).astype(jnp.bfloat16)
    partner_is = owned[:, 1][:, None] == clips[None, :]
    partner_slot = jnp.sum(jnp.where(partner_is, owned_rank[None, :], 0), axis=1)
    source = (owned[:, 1] // clip_count - owner + owners) % owners
    partner_slot = partner_slot + source * slots
    partner_hot = (
        partner_slot[:, None] == jnp.arange(owners * slots, dtype=jnp.int32)[None, :]
    ).astype(jnp.bfloat16)

    first_rows = dot(
        first_hot, firsts.reshape(clip_count, row_width), ((1,), (0,)), jnp.bfloat16
    ).reshape(times, per_device, block, feature)
    partner_rows = dot(
        partner_hot, partners.reshape(owners * slots, row_width), ((1,), (0,)), jnp.bfloat16
    ).reshape(times, per_device, block, feature)
    rows = jnp.concatenate([first_rows, partner_rows], axis=1)
    rows = rows.reshape(times, 2 * per_device * block, feature)
    frames = lax.all_to_all(rows, both, 0, 0, axis_index_groups=home, tiled=True)
    frames = frames.reshape(times, 2, per_device, block, feature).transpose(1, 2, 0, 3, 4)
    frames = frames.reshape(2, per_device, times * block, feature)

    my_ids = lax.dynamic_slice_in_dim(owned, place * per_device, per_device, 0)
    len_first = jnp.take(lengths, my_ids[:, 0])
    len_partner = jnp.take(lengths, my_ids[:, 1])
    losses, grad_first, grad_partner = jax.vmap(pair_grads)(
        frames[0], frames[1], len_first, len_partner, weight
    )

    grads = jnp.stack([grad_first, grad_partner]).reshape(
        2, per_device, times, block, feature
    )
    grads = grads.transpose(2, 0, 1, 3, 4).reshape(times, 2 * per_device * block, feature)
    returned = lax.all_to_all(grads, both, 0, 0, axis_index_groups=home, tiled=True)
    returned = returned.reshape(times, 2, per_device, row_width)
    first_back = returned[:, 0].reshape(per_owner, row_width)
    partner_back = returned[:, 1].reshape(per_owner, row_width)
    first_sum = dot(first_hot, first_back, ((0,), (0,))).astype(jnp.bfloat16)
    first_sum = with_scalars(first_sum.reshape(clip_count * block, feature), losses)
    first_sum = lax.ppermute(first_sum, both, back)
    partner_sum = dot(partner_hot, partner_back, ((0,), (0,))).astype(jnp.bfloat16)
    partner_sum = partner_sum.reshape(owners, slots * block, feature)
    partner_sum = lax.all_to_all(partner_sum, both, 0, 0, axis_index_groups=plane, tiled=True)
    first_sum, losses = without_scalars(first_sum, per_device)
    partner_sum = lax.all_to_all(
        partner_sum, "tm", 0, 0, axis_index_groups=long_range, tiled=True
    )
    total = dot(chosen, partner_sum.reshape(owners * slots, row_width), ((0,), (0,)))
    total = total.reshape(clip_count, block, feature)
    total = total + first_sum.reshape(clip_count, block, feature).astype(jnp.float32)
    unit = as_float * scale
    gradient = scale * (total - unit * jnp.mean(total * unit, axis=-1, keepdims=True))
    return (losses, gradient.astype(jnp.bfloat16))


def solution(mesh):
    in_specs = (P("clip", "tm", None), P(), P(), P(("clip", "tm")))
    out_specs = (P(("clip", "tm")), P("clip", "tm", None))
    return jax.shard_map(shards, mesh=mesh, in_specs=in_specs, out_specs=out_specs, check_vma=False)
```

```python
import functools
import math

import jax
import jax.numpy as jnp
from jax import lax
from jax.experimental import pallas as pl
from jax.experimental.pallas import tpu as pltpu
from jax.sharding import PartitionSpec as P

score_scale = 2.0
spread_floor = 1.0
log_weight = 0.1
epsilon = 1e-06
slots = 4


def dot(left, right, contract, out=jnp.float32):
    return lax.dot_general(left, right, (contract, ((), ())), preferred_element_type=out)


def split(values, parts):
    pieces = []
    for _ in range(parts):
        piece = lax.reduce_precision(values, 8, 7)
        pieces.append(piece.astype(jnp.bfloat16))
        values = values - piece
    return pieces


def with_scalars(rows, scalars):
    pieces = jnp.stack(split(scalars, 3))
    pad = ((0, 8 - pieces.shape[0]), (0, rows.shape[1] - pieces.shape[1]))
    return jnp.concatenate([rows, jnp.pad(pieces, pad)], axis=0)


def without_scalars(packed, count):
    pieces = packed[-8:-5, :count].astype(jnp.float32)
    return packed[:-8], (pieces[0] + pieces[1]) + pieces[2]


def pair_math(n_first, n_partner, len_first, len_partner, weight, row_time, column_time):
    factor = score_scale / math.sqrt(n_first.shape[1])
    scores = dot(n_first, n_partner, ((1,), (1,))) * factor
    forward_exp = jnp.where(column_time < len_partner, jnp.exp(scores), 0.0)
    forward_prob = forward_exp / jnp.sum(forward_exp, axis=1, keepdims=True)
    prob = forward_prob.astype(jnp.bfloat16)
    high = scores.astype(jnp.bfloat16)
    low = (scores - high.astype(jnp.float32)).astype(jnp.bfloat16)
    backward_scores = dot(prob, high, ((1,), (1,))) + dot(prob, low, ((1,), (1,)))
    backward_exp = jnp.where(column_time < len_first, jnp.exp(backward_scores), 0.0)
    back_prob = backward_exp / jnp.sum(backward_exp, axis=1, keepdims=True)
    mean_time = jnp.sum(back_prob * column_time, axis=1, keepdims=True)
    offsets = column_time - mean_time
    squares = offsets * offsets
    variance = jnp.sum(back_prob * squares, axis=1, keepdims=True)
    spread = variance + spread_floor
    missed = row_time - mean_time
    ratio = missed / spread
    terms = missed * ratio + log_weight * jnp.log(spread)
    valid = row_time < len_first
    loss = jnp.sum(jnp.where(valid, terms, 0.0)) / len_first
    row_weight = jnp.where(valid, weight / len_first, 0.0)
    d_mean = -2.0 * ratio * row_weight
    d_spread = (log_weight / spread - ratio * ratio) * row_weight
    d_back = back_prob * (d_mean * offsets + d_spread * (squares - variance))
    d_low = d_back.astype(jnp.bfloat16)
    d_prob = dot(d_low, high, ((1,), (0,))) + dot(d_low, low, ((1,), (0,)))
    d_scores = forward_prob * (d_prob - jnp.sum(forward_prob * d_prob, axis=1, keepdims=True))
    d_scores = d_scores + dot(d_back.T.astype(jnp.bfloat16), prob, ((1,), (0,)))
    d_scores = d_scores * factor
    grad_first = dot(d_scores.astype(jnp.bfloat16), n_partner, ((1,), (0,)))
    grad_partner = dot(d_scores.T.astype(jnp.bfloat16), n_first, ((1,), (0,)))
    return loss, grad_first, grad_partner


def pair_kernel(block, weights, length_ref, weight_ref, rows_ref, out_ref, loss_ref, wide):
    total = rows_ref.shape[0]
    count = weights
    chunk = 2 * count * block
    sources = total // chunk
    frames = sources * block
    lanes = wide.shape[2]
    strips = wide.shape[0]
    for c in range(strips):
        wide[c] = rows_ref[:, c * lanes : (c + 1) * lanes].astype(jnp.float32)
    row = lax.broadcasted_iota(jnp.int32, (frames, 1), 0)
    row_time = ((row % sources) * block + row // sources).astype(jnp.float32)
    column = lax.broadcasted_iota(jnp.int32, (1, frames), 1)
    column_time = ((column % sources) * block + column // sources).astype(jnp.float32)

    def place(kind, pair, frame):
        return pl.ds((kind * count + pair) * block + frame, sources, stride=chunk)

    for pair in range(count):
        clips = [
            jnp.concatenate(
                [
                    jnp.concatenate(
                        [wide[c, place(kind, pair, f), :] for f in range(block)], axis=0
                    ).astype(jnp.bfloat16)
                    for c in range(strips)
                ],
                axis=1,
            )
            for kind in range(2)
        ]
        loss, *grads = pair_math(
            clips[0],
            clips[1],
            length_ref[0, pair].astype(jnp.float32),
            length_ref[1, pair].astype(jnp.float32),
            weight_ref[pair],
            row_time,
            column_time,
        )
        loss_ref[pair] = loss
        for kind in range(2):
            for f in range(block):
                part = grads[kind][f * sources : (f + 1) * sources]
                for c in range(strips):
                    wide[c, place(kind, pair, f), :] = part[:, c * lanes : (c + 1) * lanes]
    for c in range(strips):
        out_ref[:, c * lanes : (c + 1) * lanes] = wide[c].astype(jnp.bfloat16)


def pair_call(rows, lengths, weight, block):
    smem = pl.BlockSpec(memory_space=pltpu.SMEM)
    vmem = pl.BlockSpec(memory_space=pltpu.VMEM)
    return pl.pallas_call(
        functools.partial(pair_kernel, block, weight.shape[0]),
        out_shape=(
            jax.ShapeDtypeStruct(rows.shape, jnp.bfloat16),
            jax.ShapeDtypeStruct(weight.shape, jnp.float32),
        ),
        in_specs=[smem, smem, vmem],
        out_specs=(vmem, smem),
        scratch_shapes=[pltpu.VMEM((rows.shape[1] // 128, rows.shape[0], 128), jnp.float32)],
        compiler_params=pltpu.CompilerParams(vmem_limit_bytes=40 * 1024 * 1024),
    )(lengths, weight, rows)


def spread_rows(hot, block):
    rows = jnp.arange(hot.shape[0] * block, dtype=jnp.int32)
    columns = jnp.arange(hot.shape[1] * block, dtype=jnp.int32)
    same = rows[:, None] % block == columns[None, :] % block
    wide = jnp.repeat(jnp.repeat(hot, block, axis=0), block, axis=1)
    return jnp.where(same, wide, 0).astype(jnp.bfloat16)


def shards(embeddings, lengths, pairs, scaled_weight):
    owners = lax.axis_size("clip")
    times = lax.axis_size("tm")
    clip_count, block, feature = embeddings.shape
    per_device = scaled_weight.shape[0]
    per_owner = per_device * times
    row_width = block * feature
    spots = times // owners
    column = lax.axis_index("clip")
    time_index = lax.axis_index("tm")
    owner = time_index // spots
    spot = time_index % spots
    turn = (column - owner + owners) % owners
    place = turn * spots + spot

    long_range = [[a + spots * i for i in range(owners)] for a in range(spots)]
    home = [
        [((m + c) % owners) * times + spots * c + q for m in range(owners) for q in range(spots)]
        for c in range(owners)
    ]
    plane = [
        [((m + t // spots) % owners) * times + t for m in range(owners)] for t in range(times)
    ]
    swap = [
        (c * times + t, ((t // spots + c) % owners) * times + c * spots + t % spots)
        for c in range(owners)
        for t in range(times)
    ]
    back = [(there, here) for here, there in swap]
    both = ("clip", "tm")

    as_float = embeddings.astype(jnp.float32)
    scale = lax.rsqrt(jnp.mean(as_float * as_float, axis=-1, keepdims=True) + epsilon)
    normalized = (as_float * scale).astype(jnp.bfloat16).reshape(clip_count * block, feature)

    packed = with_scalars(normalized, scaled_weight)

    grouped = pairs.reshape(owners, per_owner, 2)
    clips = jnp.arange(owners * clip_count, dtype=jnp.int32)
    used = jnp.any(grouped[:, :, 1, None] == clips[None, None, :], axis=1)
    before = (clips[:, None] // clip_count == clips[None, :] // clip_count) & (
        clips[:, None] < clips[None, :]
    )
    rank = dot(used.astype(jnp.bfloat16), before.astype(jnp.bfloat16), ((1,), (0,)))
    rank = jnp.where(used, rank.astype(jnp.int32), -1)
    mine = lax.dynamic_slice_in_dim(rank, column * clip_count, clip_count, 1)
    slot_ids = jnp.arange(slots, dtype=jnp.int32)
    chosen = mine[:, None, :] == slot_ids[None, :, None]
    chosen = chosen.reshape(owners * slots, clip_count).astype(jnp.bfloat16)

    outgoing = dot(
        spread_rows(chosen, block), normalized, ((1,), (0,)), jnp.bfloat16
    ).reshape(owners, slots * block, feature)
    outgoing = lax.all_to_all(
        outgoing, "tm", 0, 0, axis_index_groups=long_range, tiled=True
    )
    firsts, weight = without_scalars(lax.ppermute(packed, both, swap), per_device)
    partners = lax.all_to_all(outgoing, both, 0, 0, axis_index_groups=plane, tiled=True)

    owned = lax.dynamic_index_in_dim(grouped, owner, 0, keepdims=False)
    owned_rank = lax.dynamic_index_in_dim(rank, owner, 0, keepdims=False)
    first_slot = owned[:, 0] - owner * clip_count
    partner_is = owned[:, 1][:, None] == clips[None, :]
    partner_slot = jnp.sum(jnp.where(partner_is, owned_rank[None, :], 0), axis=1)
    source = (owned[:, 1] // clip_count - owner + owners) % owners
    partner_slot = partner_slot + source * slots
    slot_of = jnp.stack(
        [first_slot.reshape(times, per_device), partner_slot.reshape(times, per_device)], axis=1
    ).reshape(-1)
    row_count = 2 * per_owner * block
    row_slot = jnp.repeat(slot_of, block)
    row_index = jnp.arange(row_count, dtype=jnp.int32)
    row_key = row_slot * block + row_index % block
    is_first = (row_index // (per_device * block)) % 2 == 0
    first_key = jnp.where(is_first, row_key, -1)
    partner_key = jnp.where(is_first, -1, row_key)
    first_spots = jnp.arange(clip_count * block, dtype=jnp.int32)
    partner_spots = jnp.arange(owners * slots * block, dtype=jnp.int32)
    first_hot = (first_key[:, None] == first_spots[None, :]).astype(jnp.bfloat16)
    partner_hot = (partner_key[:, None] == partner_spots[None, :]).astype(jnp.bfloat16)
    first_back = (first_spots[:, None] == first_key[None, :]).astype(jnp.bfloat16)
    partner_back = (partner_spots[:, None] == partner_key[None, :]).astype(jnp.bfloat16)

    rows = dot(first_hot, firsts, ((1,), (0,)))
    rows = rows + dot(partner_hot, partners.reshape(-1, feature), ((1,), (0,)))
    rows = rows.astype(jnp.bfloat16).reshape(times, 2 * per_device * block, feature)
    rows = lax.all_to_all(rows, both, 0, 0, axis_index_groups=home, tiled=True)

    my_ids = lax.dynamic_slice_in_dim(owned, place * per_device, per_device, 0)
    pair_lengths = jnp.take(lengths, my_ids.T)
    grads, losses = pair_call(rows.reshape(row_count, feature), pair_lengths, weight, block)

    grads = grads.reshape(times, 2 * per_device * block, feature)
    returned = lax.all_to_all(grads, both, 0, 0, axis_index_groups=home, tiled=True)
    returned = returned.reshape(row_count, feature)
    partner_sum = dot(partner_back, returned, ((1,), (0,))).astype(jnp.bfloat16)
    first_sum = dot(first_back, returned, ((1,), (0,))).astype(jnp.bfloat16)
    first_sum = with_scalars(first_sum, losses)
    first_sum = lax.ppermute(first_sum, both, back)
    partner_sum = partner_sum.reshape(owners, slots * block, feature)
    partner_sum = lax.all_to_all(partner_sum, both, 0, 0, axis_index_groups=plane, tiled=True)
    first_sum, losses = without_scalars(first_sum, per_device)
    partner_sum = lax.all_to_all(
        partner_sum, "tm", 0, 0, axis_index_groups=long_range, tiled=True
    )
    total = dot(spread_rows(chosen.T, block), partner_sum.reshape(-1, feature), ((1,), (0,)))
    total = (total + first_sum.astype(jnp.float32)).reshape(clip_count, block, feature)
    unit = as_float * scale
    gradient = scale * (total - unit * jnp.mean(total * unit, axis=-1, keepdims=True))
    return (losses, gradient.astype(jnp.bfloat16))


def solution(mesh):
    in_specs = (P("clip", "tm", None), P(), P(), P(("clip", "tm")))
    out_specs = (P(("clip", "tm")), P("clip", "tm", None))
    return jax.shard_map(shards, mesh=mesh, in_specs=in_specs, out_specs=out_specs, check_vma=False)
```

```python
import functools
import math

import jax
import jax.numpy as jnp
from jax import lax
from jax.experimental import pallas as pl
from jax.experimental.pallas import tpu as pltpu
from jax.sharding import PartitionSpec as P

score_scale = 2.0
spread_floor = 1.0
log_weight = 0.1
epsilon = 1e-06
slots = 4


def dot(left, right, contract, out=jnp.float32):
    return lax.dot_general(left, right, (contract, ((), ())), preferred_element_type=out)


def split(values, parts):
    pieces = []
    for _ in range(parts):
        piece = lax.reduce_precision(values, 8, 7)
        pieces.append(piece.astype(jnp.bfloat16))
        values = values - piece
    return pieces


def with_scalars(rows, scalars):
    pieces = jnp.stack(split(scalars, 3))
    pad = ((0, 8 - pieces.shape[0]), (0, rows.shape[1] - pieces.shape[1]))
    return jnp.concatenate([rows, jnp.pad(pieces, pad)], axis=0)


def without_scalars(packed, count):
    pieces = packed[-8:-5, :count].astype(jnp.float32)
    return packed[:-8], (pieces[0] + pieces[1]) + pieces[2]


def pair_math(n_first, n_partner, len_first, len_partner, weight, row_time, column_time):
    factor = score_scale / math.sqrt(n_first.shape[1])
    scores = dot(n_first, n_partner, ((1,), (1,))) * factor
    forward_exp = jnp.where(column_time < len_partner, jnp.exp(scores), 0.0)
    forward_prob = forward_exp / jnp.sum(forward_exp, axis=1, keepdims=True)
    prob = forward_prob.astype(jnp.bfloat16)
    high = scores.astype(jnp.bfloat16)
    low = (scores - high.astype(jnp.float32)).astype(jnp.bfloat16)
    backward_scores = dot(prob, high, ((1,), (1,))) + dot(prob, low, ((1,), (1,)))
    backward_exp = jnp.where(column_time < len_first, jnp.exp(backward_scores), 0.0)
    back_prob = backward_exp / jnp.sum(backward_exp, axis=1, keepdims=True)
    mean_time = jnp.sum(back_prob * column_time, axis=1, keepdims=True)
    offsets = column_time - mean_time
    squares = offsets * offsets
    variance = jnp.sum(back_prob * squares, axis=1, keepdims=True)
    spread = variance + spread_floor
    missed = row_time - mean_time
    ratio = missed / spread
    terms = missed * ratio + log_weight * jnp.log(spread)
    valid = row_time < len_first
    loss = jnp.sum(jnp.where(valid, terms, 0.0)) / len_first
    row_weight = jnp.where(valid, weight / len_first, 0.0)
    d_mean = -2.0 * ratio * row_weight
    d_spread = (log_weight / spread - ratio * ratio) * row_weight
    d_back = back_prob * (d_mean * offsets + d_spread * (squares - variance))
    d_low = d_back.astype(jnp.bfloat16)
    d_prob = dot(d_low, high, ((1,), (0,))) + dot(d_low, low, ((1,), (0,)))
    d_scores = forward_prob * (d_prob - jnp.sum(forward_prob * d_prob, axis=1, keepdims=True))
    d_scores = d_scores + dot(d_back.T.astype(jnp.bfloat16), prob, ((1,), (0,)))
    d_scores = d_scores * factor
    grad_first = dot(d_scores.astype(jnp.bfloat16), n_partner, ((1,), (0,)))
    grad_partner = dot(d_scores.T.astype(jnp.bfloat16), n_first, ((1,), (0,)))
    return loss, grad_first, grad_partner


def pair_kernel(block, weights, length_ref, weight_ref, rows_ref, out_ref, loss_ref, wide):
    total = rows_ref.shape[0]
    count = weights
    chunk = 2 * count * block
    sources = total // chunk
    frames = sources * block
    lanes = wide.shape[2]
    strips = wide.shape[0]
    for c in range(strips):
        wide[c] = rows_ref[:, c * lanes : (c + 1) * lanes].astype(jnp.float32)
    row = lax.broadcasted_iota(jnp.int32, (frames, 1), 0)
    row_time = ((row % sources) * block + row // sources).astype(jnp.float32)
    column = lax.broadcasted_iota(jnp.int32, (1, frames), 1)
    column_time = ((column % sources) * block + column // sources).astype(jnp.float32)

    def place(kind, pair, frame):
        return pl.ds((kind * count + pair) * block + frame, sources, stride=chunk)

    for pair in range(count):
        clips = [
            jnp.concatenate(
                [
                    jnp.concatenate(
                        [wide[c, place(kind, pair, f), :] for f in range(block)], axis=0
                    ).astype(jnp.bfloat16)
                    for c in range(strips)
                ],
                axis=1,
            )
            for kind in range(2)
        ]
        loss, *grads = pair_math(
            clips[0],
            clips[1],
            length_ref[0, pair].astype(jnp.float32),
            length_ref[1, pair].astype(jnp.float32),
            weight_ref[pair],
            row_time,
            column_time,
        )
        loss_ref[pair] = loss
        for kind in range(2):
            for f in range(block):
                part = grads[kind][f * sources : (f + 1) * sources]
                for c in range(strips):
                    wide[c, place(kind, pair, f), :] = part[:, c * lanes : (c + 1) * lanes]
    for c in range(strips):
        out_ref[:, c * lanes : (c + 1) * lanes] = wide[c].astype(jnp.bfloat16)


def pair_call(rows, lengths, weight, block):
    smem = pl.BlockSpec(memory_space=pltpu.SMEM)
    vmem = pl.BlockSpec(memory_space=pltpu.VMEM)
    return pl.pallas_call(
        functools.partial(pair_kernel, block, weight.shape[0]),
        out_shape=(
            jax.ShapeDtypeStruct(rows.shape, jnp.bfloat16),
            jax.ShapeDtypeStruct(weight.shape, jnp.float32),
        ),
        in_specs=[smem, smem, vmem],
        out_specs=(vmem, smem),
        scratch_shapes=[pltpu.VMEM((rows.shape[1] // 128, rows.shape[0], 128), jnp.float32)],
        compiler_params=pltpu.CompilerParams(vmem_limit_bytes=40 * 1024 * 1024),
    )(lengths, weight, rows)


def spread_rows(hot, block):
    rows = jnp.arange(hot.shape[0] * block, dtype=jnp.int32)
    columns = jnp.arange(hot.shape[1] * block, dtype=jnp.int32)
    same = rows[:, None] % block == columns[None, :] % block
    wide = jnp.repeat(jnp.repeat(hot, block, axis=0), block, axis=1)
    return jnp.where(same, wide, 0).astype(jnp.bfloat16)


def shards(embeddings, lengths, pairs, scaled_weight):
    owners = lax.axis_size("clip")
    times = lax.axis_size("tm")
    clip_count, block, feature = embeddings.shape
    per_device = scaled_weight.shape[0]
    per_owner = per_device * times
    row_width = block * feature
    spots = times // owners
    column = lax.axis_index("clip")
    time_index = lax.axis_index("tm")
    owner = time_index // spots
    spot = time_index % spots
    turn = (column - owner + owners) % owners
    place = turn * spots + spot

    long_range = [[a + spots * i for i in range(owners)] for a in range(spots)]
    home = [
        [((m + c) % owners) * times + spots * c + q for m in range(owners) for q in range(spots)]
        for c in range(owners)
    ]
    plane = [
        [((m + t // spots) % owners) * times + t for m in range(owners)] for t in range(times)
    ]
    swap = [
        (c * times + t, ((t // spots + c) % owners) * times + c * spots + t % spots)
        for c in range(owners)
        for t in range(times)
    ]
    back = [(there, here) for here, there in swap]
    both = ("clip", "tm")

    as_float = embeddings.astype(jnp.float32)
    scale = lax.rsqrt(jnp.mean(as_float * as_float, axis=-1, keepdims=True) + epsilon)
    normalized = (as_float * scale).astype(jnp.bfloat16).reshape(clip_count * block, feature)

    spread = lax.all_to_all(
        normalized.reshape(clip_count, block, feature), "clip", 0, 0, tiled=True
    ).reshape(clip_count * block, feature)
    weight = lax.ppermute(scaled_weight, both, swap)
    spread, weight = lax.optimization_barrier((spread, weight))

    grouped = pairs.reshape(owners, per_owner, 2)
    clips = jnp.arange(owners * clip_count, dtype=jnp.int32)
    used = jnp.any(grouped[:, :, 1, None] == clips[None, None, :], axis=1)
    before = (clips[:, None] // clip_count == clips[None, :] // clip_count) & (
        clips[:, None] < clips[None, :]
    )
    rank = dot(used.astype(jnp.bfloat16), before.astype(jnp.bfloat16), ((1,), (0,)))
    rank = jnp.where(used, rank.astype(jnp.int32), -1)
    mine = lax.dynamic_slice_in_dim(rank, column * clip_count, clip_count, 1)
    slot_ids = jnp.arange(slots, dtype=jnp.int32)
    chosen = mine[:, None, :] == slot_ids[None, :, None]
    chosen = chosen.reshape(owners * slots, clip_count).astype(jnp.bfloat16)

    depth = (slots + 1) * block
    half = feature // 2
    own = jnp.where(jnp.eye(owners, dtype=bool), slots, -1)
    wanted = jnp.concatenate([mine, own], axis=1).astype(jnp.bfloat16)
    out_row = jnp.arange(owners * 2 * depth, dtype=jnp.int32)
    in_row = jnp.arange(2 * clip_count * block, dtype=jnp.int32)
    of_owner = out_row[:, None] // (2 * depth) == jnp.arange(owners, dtype=jnp.int32)[None, :]
    of_source = jnp.arange(2 * clip_count, dtype=jnp.int32)[:, None] == in_row[None, :] // block
    wanted = dot(of_owner.astype(jnp.bfloat16), wanted, ((1,), (0,)), jnp.bfloat16)
    wanted = dot(wanted, of_source.astype(jnp.bfloat16), ((1,), (0,))).astype(jnp.int32)
    out_depth = out_row % depth
    picked = (wanted == out_depth[:, None] // block) & (
        out_depth[:, None] % block == in_row[None, :] % block
    )
    picked = picked.astype(jnp.bfloat16)
    sources = jnp.concatenate([normalized, spread], axis=0)
    upper = (out_row % (2 * depth) >= depth)[:, None]
    outgoing = jnp.where(
        upper,
        dot(picked, sources[:, half:], ((1,), (0,))),
        dot(picked, sources[:, :half], ((1,), (0,))),
    )
    outgoing = outgoing.astype(jnp.bfloat16).reshape(owners, 2 * depth, half)
    outgoing = lax.all_to_all(
        outgoing, "tm", 0, 0, axis_index_groups=long_range, tiled=True
    )
    partners = lax.all_to_all(outgoing, both, 0, 0, axis_index_groups=plane, tiled=True)
    partners = partners.reshape(owners * 2 * depth, half)

    owned = lax.dynamic_index_in_dim(grouped, owner, 0, keepdims=False)
    owned_rank = lax.dynamic_index_in_dim(rank, owner, 0, keepdims=False)
    first_slot = owned[:, 0] - owner * clip_count
    partner_is = owned[:, 1][:, None] == clips[None, :]
    partner_slot = jnp.sum(jnp.where(partner_is, owned_rank[None, :], 0), axis=1)
    source = (owned[:, 1] // clip_count - owner + owners) % owners
    partner_slot = partner_slot + source * slots
    slot_of = jnp.stack(
        [first_slot.reshape(times, per_device), partner_slot.reshape(times, per_device)], axis=1
    ).reshape(-1)
    row_count = 2 * per_owner * block
    row_slot = jnp.repeat(slot_of, block)
    row_index = jnp.arange(row_count, dtype=jnp.int32)
    row_key = row_slot * block + row_index % block
    is_first = (row_index // (per_device * block)) % 2 == 0
    first_key = jnp.where(is_first, row_key, -1)
    partner_key = jnp.where(is_first, -1, row_key)
    first_spots = jnp.arange(clip_count * block, dtype=jnp.int32)
    partner_spots = jnp.arange(owners * slots * block, dtype=jnp.int32)
    first_back = (first_spots[:, None] == first_key[None, :]).astype(jnp.bfloat16)
    partner_back = (partner_spots[:, None] == partner_key[None, :]).astype(jnp.bfloat16)

    first_source = (first_slot - owner + owners * clip_count) % owners
    entry_of = jnp.stack(
        [
            (first_source * 2 * depth + slots * block).reshape(times, per_device),
            (source * 2 * depth + (partner_slot % slots) * block).reshape(times, per_device),
        ],
        axis=1,
    ).reshape(-1)
    entry = (jnp.repeat(entry_of, block) + row_index % block)[:, None]
    entries = jnp.arange(owners * 2 * depth, dtype=jnp.int32)[None, :]
    lower_rows = dot((entry == entries).astype(jnp.bfloat16), partners, ((1,), (0,)))
    upper_rows = dot((entry + depth == entries).astype(jnp.bfloat16), partners, ((1,), (0,)))
    rows = jnp.concatenate([lower_rows, upper_rows], axis=1)
    rows = rows.astype(jnp.bfloat16).reshape(times, 2 * per_device * block, feature)
    rows = lax.all_to_all(rows, both, 0, 0, axis_index_groups=home, tiled=True)

    my_ids = lax.dynamic_slice_in_dim(owned, place * per_device, per_device, 0)
    pair_lengths = jnp.take(lengths, my_ids.T)
    grads, losses = pair_call(rows.reshape(row_count, feature), pair_lengths, weight, block)

    grads = grads.reshape(times, 2 * per_device * block, feature)
    returned = lax.all_to_all(grads, both, 0, 0, axis_index_groups=home, tiled=True)
    returned = returned.reshape(row_count, feature)
    partner_sum = dot(partner_back, returned, ((1,), (0,))).astype(jnp.bfloat16)
    first_sum = dot(first_back, returned, ((1,), (0,))).astype(jnp.bfloat16)
    first_sum = with_scalars(first_sum, losses)
    first_sum = lax.ppermute(first_sum, both, back)
    partner_sum = partner_sum.reshape(owners, slots * block, feature)
    partner_sum = lax.all_to_all(partner_sum, both, 0, 0, axis_index_groups=plane, tiled=True)
    first_sum, losses = without_scalars(first_sum, per_device)
    partner_sum = lax.all_to_all(
        partner_sum, "tm", 0, 0, axis_index_groups=long_range, tiled=True
    )
    total = dot(spread_rows(chosen.T, block), partner_sum.reshape(-1, feature), ((1,), (0,)))
    total = (total + first_sum.astype(jnp.float32)).reshape(clip_count, block, feature)
    unit = as_float * scale
    gradient = scale * (total - unit * jnp.mean(total * unit, axis=-1, keepdims=True))
    return (losses, gradient.astype(jnp.bfloat16))


def solution(mesh):
    in_specs = (P("clip", "tm", None), P(), P(), P(("clip", "tm")))
    out_specs = (P(("clip", "tm")), P("clip", "tm", None))
    return jax.shard_map(shards, mesh=mesh, in_specs=in_specs, out_specs=out_specs, check_vma=False)
```

```python
import functools
import math

import jax
import jax.numpy as jnp
from jax import lax
from jax.experimental import pallas as pl
from jax.experimental.pallas import tpu as pltpu
from jax.sharding import PartitionSpec as P

score_scale = 2.0
spread_floor = 1.0
log_weight = 0.1
epsilon = 1e-06
slots = 4


def dot(left, right, contract, out=jnp.float32):
    return lax.dot_general(left, right, (contract, ((), ())), preferred_element_type=out)


def split(values, parts):
    pieces = []
    for _ in range(parts):
        piece = lax.reduce_precision(values, 8, 7)
        pieces.append(piece.astype(jnp.bfloat16))
        values = values - piece
    return pieces


def with_scalars(rows, scalars):
    pieces = jnp.stack(split(scalars, 3))
    pad = ((0, 8 - pieces.shape[0]), (0, rows.shape[1] - pieces.shape[1]))
    return jnp.concatenate([rows, jnp.pad(pieces, pad)], axis=0)


def without_scalars(packed, count):
    pieces = packed[-8:-5, :count].astype(jnp.float32)
    return packed[:-8], (pieces[0] + pieces[1]) + pieces[2]


def pair_math(n_first, n_partner, len_first, len_partner, weight, row_time, column_time):
    factor = score_scale / math.sqrt(n_first.shape[1])
    scores = dot(n_first, n_partner, ((1,), (1,))) * factor
    forward_exp = jnp.where(column_time < len_partner, jnp.exp(scores), 0.0)
    forward_prob = forward_exp / jnp.sum(forward_exp, axis=1, keepdims=True)
    prob = forward_prob.astype(jnp.bfloat16)
    high = scores.astype(jnp.bfloat16)
    low = (scores - high.astype(jnp.float32)).astype(jnp.bfloat16)
    backward_scores = dot(prob, high, ((1,), (1,))) + dot(prob, low, ((1,), (1,)))
    backward_exp = jnp.where(column_time < len_first, jnp.exp(backward_scores), 0.0)
    back_prob = backward_exp / jnp.sum(backward_exp, axis=1, keepdims=True)
    mean_time = jnp.sum(back_prob * column_time, axis=1, keepdims=True)
    offsets = column_time - mean_time
    squares = offsets * offsets
    variance = jnp.sum(back_prob * squares, axis=1, keepdims=True)
    spread = variance + spread_floor
    missed = row_time - mean_time
    ratio = missed / spread
    terms = missed * ratio + log_weight * jnp.log(spread)
    valid = row_time < len_first
    loss = jnp.sum(jnp.where(valid, terms, 0.0)) / len_first
    row_weight = jnp.where(valid, weight / len_first, 0.0)
    d_mean = -2.0 * ratio * row_weight
    d_spread = (log_weight / spread - ratio * ratio) * row_weight
    d_back = back_prob * (d_mean * offsets + d_spread * (squares - variance))
    d_low = d_back.astype(jnp.bfloat16)
    d_prob = dot(d_low, high, ((1,), (0,))) + dot(d_low, low, ((1,), (0,)))
    d_scores = forward_prob * (d_prob - jnp.sum(forward_prob * d_prob, axis=1, keepdims=True))
    d_scores = d_scores + dot(d_back.T.astype(jnp.bfloat16), prob, ((1,), (0,)))
    d_scores = d_scores * factor
    grad_first = dot(d_scores.astype(jnp.bfloat16), n_partner, ((1,), (0,)))
    grad_partner = dot(d_scores.T.astype(jnp.bfloat16), n_first, ((1,), (0,)))
    return loss, grad_first, grad_partner


def pair_kernel(block, weights, length_ref, weight_ref, rows_ref, out_ref, loss_ref, wide):
    total = rows_ref.shape[0]
    count = weights
    chunk = 2 * count * block
    sources = total // chunk
    frames = sources * block
    lanes = wide.shape[2]
    strips = wide.shape[0]
    for c in range(strips):
        wide[c] = rows_ref[:, c * lanes : (c + 1) * lanes].astype(jnp.float32)
    row = lax.broadcasted_iota(jnp.int32, (frames, 1), 0)
    row_time = ((row % sources) * block + row // sources).astype(jnp.float32)
    column = lax.broadcasted_iota(jnp.int32, (1, frames), 1)
    column_time = ((column % sources) * block + column // sources).astype(jnp.float32)

    def place(kind, pair, frame):
        return pl.ds((kind * count + pair) * block + frame, sources, stride=chunk)

    for pair in range(count):
        clips = [
            jnp.concatenate(
                [
                    jnp.concatenate(
                        [wide[c, place(kind, pair, f), :] for f in range(block)], axis=0
                    ).astype(jnp.bfloat16)
                    for c in range(strips)
                ],
                axis=1,
            )
            for kind in range(2)
        ]
        loss, *grads = pair_math(
            clips[0],
            clips[1],
            length_ref[0, pair].astype(jnp.float32),
            length_ref[1, pair].astype(jnp.float32),
            weight_ref[pair],
            row_time,
            column_time,
        )
        loss_ref[pair] = loss
        for kind in range(2):
            for f in range(block):
                part = grads[kind][f * sources : (f + 1) * sources]
                for c in range(strips):
                    wide[c, place(kind, pair, f), :] = part[:, c * lanes : (c + 1) * lanes]
    for c in range(strips):
        out_ref[:, c * lanes : (c + 1) * lanes] = wide[c].astype(jnp.bfloat16)


def pair_call(rows, lengths, weight, block):
    smem = pl.BlockSpec(memory_space=pltpu.SMEM)
    vmem = pl.BlockSpec(memory_space=pltpu.VMEM)
    return pl.pallas_call(
        functools.partial(pair_kernel, block, weight.shape[0]),
        out_shape=(
            jax.ShapeDtypeStruct(rows.shape, jnp.bfloat16),
            jax.ShapeDtypeStruct(weight.shape, jnp.float32),
        ),
        in_specs=[smem, smem, vmem],
        out_specs=(vmem, smem),
        scratch_shapes=[pltpu.VMEM((rows.shape[1] // 128, rows.shape[0], 128), jnp.float32)],
        compiler_params=pltpu.CompilerParams(vmem_limit_bytes=40 * 1024 * 1024),
    )(lengths, weight, rows)


def spread_rows(hot, block):
    rows = jnp.arange(hot.shape[0] * block, dtype=jnp.int32)
    columns = jnp.arange(hot.shape[1] * block, dtype=jnp.int32)
    same = rows[:, None] % block == columns[None, :] % block
    wide = jnp.repeat(jnp.repeat(hot, block, axis=0), block, axis=1)
    return jnp.where(same, wide, 0).astype(jnp.bfloat16)


def shards(embeddings, lengths, pairs, scaled_weight):
    owners = lax.axis_size("clip")
    times = lax.axis_size("tm")
    clip_count, block, feature = embeddings.shape
    per_device = scaled_weight.shape[0]
    per_owner = per_device * times
    row_width = block * feature
    spots = times // owners
    column = lax.axis_index("clip")
    time_index = lax.axis_index("tm")
    owner = time_index // spots
    spot = time_index % spots
    turn = (column - owner + owners) % owners
    place = turn * spots + spot

    long_range = [[a + spots * i for i in range(owners)] for a in range(spots)]
    home = [
        [((m + c) % owners) * times + spots * c + q for m in range(owners) for q in range(spots)]
        for c in range(owners)
    ]
    plane = [
        [((m + t // spots) % owners) * times + t for m in range(owners)] for t in range(times)
    ]
    swap = [
        (c * times + t, ((t // spots + c) % owners) * times + c * spots + t % spots)
        for c in range(owners)
        for t in range(times)
    ]
    back = [(there, here) for here, there in swap]
    both = ("clip", "tm")

    as_float = embeddings.astype(jnp.float32)
    scale = lax.rsqrt(jnp.mean(as_float * as_float, axis=-1, keepdims=True) + epsilon)
    normalized = (as_float * scale).astype(jnp.bfloat16).reshape(clip_count * block, feature)

    lanes = 128
    pieces = jnp.pad(jnp.stack(split(scaled_weight, 3)).reshape(-1), (0, lanes - 3 * per_device))
    tail = jnp.broadcast_to(pieces, (clip_count, block, lanes))
    spread = jnp.concatenate([normalized.reshape(clip_count, block, feature), tail], axis=2)
    spread = lax.all_to_all(spread, "clip", 0, 0, tiled=True)
    weight_rows = spread[:, 0, feature:]
    spread = spread[:, :, :feature].reshape(clip_count * block, feature)

    grouped = pairs.reshape(owners, per_owner, 2)
    clips = jnp.arange(owners * clip_count, dtype=jnp.int32)
    used = jnp.any(grouped[:, :, 1, None] == clips[None, None, :], axis=1)
    before = (clips[:, None] // clip_count == clips[None, :] // clip_count) & (
        clips[:, None] < clips[None, :]
    )
    rank = dot(used.astype(jnp.bfloat16), before.astype(jnp.bfloat16), ((1,), (0,)))
    rank = jnp.where(used, rank.astype(jnp.int32), -1)
    mine = lax.dynamic_slice_in_dim(rank, column * clip_count, clip_count, 1)
    slot_ids = jnp.arange(slots, dtype=jnp.int32)
    chosen = mine[:, None, :] == slot_ids[None, :, None]
    chosen = chosen.reshape(owners * slots, clip_count).astype(jnp.bfloat16)

    depth = (slots + 1) * block
    parts = 3
    width = feature // parts
    chunk = -(-parts * depth // 16) * 16
    own = jnp.where(jnp.eye(owners, dtype=bool), slots, -1)
    wanted = jnp.concatenate([mine, own], axis=1).astype(jnp.bfloat16)
    out_row = jnp.arange(owners * chunk, dtype=jnp.int32)
    in_row = jnp.arange(2 * clip_count * block, dtype=jnp.int32)
    of_owner = out_row[:, None] // chunk == jnp.arange(owners, dtype=jnp.int32)[None, :]
    of_source = jnp.arange(2 * clip_count, dtype=jnp.int32)[:, None] == in_row[None, :] // block
    wanted = dot(of_owner.astype(jnp.bfloat16), wanted, ((1,), (0,)), jnp.bfloat16)
    wanted = dot(wanted, of_source.astype(jnp.bfloat16), ((1,), (0,))).astype(jnp.int32)
    out_part = (out_row % chunk // depth)[:, None]
    out_depth = (out_row % chunk % depth)[:, None]
    picked = (wanted == out_depth // block) & (out_depth % block == in_row[None, :] % block)
    pick = [picked & (out_part == h) for h in range(parts)]
    pick.append(of_owner & (out_part == parts) & (out_depth == 0))
    pick = jnp.concatenate(pick, axis=1).astype(jnp.bfloat16)
    sources = jnp.concatenate([normalized, spread], axis=0)
    sources = [sources[:, h * width : (h + 1) * width] for h in range(parts)]
    sources.append(jnp.pad(weight_rows, ((0, 0), (0, width - lanes))))
    outgoing = dot(pick, jnp.concatenate(sources, axis=0), ((1,), (0,)), jnp.bfloat16)
    outgoing = outgoing.reshape(owners, chunk, width)
    outgoing = lax.all_to_all(
        outgoing, "tm", 0, 0, axis_index_groups=long_range, tiled=True
    )
    partners = lax.all_to_all(outgoing, both, 0, 0, axis_index_groups=plane, tiled=True)
    pieces = partners[0, parts * depth, : 3 * per_device].astype(jnp.float32)
    pieces = pieces.reshape(3, per_device)
    weight = (pieces[0] + pieces[1]) + pieces[2]
    partners = jnp.concatenate(
        [partners[:, h * depth : (h + 1) * depth] for h in range(parts)], axis=2
    ).reshape(owners * depth, feature)

    owned = lax.dynamic_index_in_dim(grouped, owner, 0, keepdims=False)
    owned_rank = lax.dynamic_index_in_dim(rank, owner, 0, keepdims=False)
    first_slot = owned[:, 0] - owner * clip_count
    partner_is = owned[:, 1][:, None] == clips[None, :]
    partner_slot = jnp.sum(jnp.where(partner_is, owned_rank[None, :], 0), axis=1)
    source = (owned[:, 1] // clip_count - owner + owners) % owners
    partner_slot = partner_slot + source * slots
    slot_of = jnp.stack(
        [first_slot.reshape(times, per_device), partner_slot.reshape(times, per_device)], axis=1
    ).reshape(-1)
    row_count = 2 * per_owner * block
    row_slot = jnp.repeat(slot_of, block)
    row_index = jnp.arange(row_count, dtype=jnp.int32)
    row_key = row_slot * block + row_index % block
    is_first = (row_index // (per_device * block)) % 2 == 0
    first_key = jnp.where(is_first, row_key, -1)
    partner_key = jnp.where(is_first, -1, row_key)
    first_spots = jnp.arange(clip_count * block, dtype=jnp.int32)
    partner_spots = jnp.arange(owners * slots * block, dtype=jnp.int32)
    first_back = (first_spots[:, None] == first_key[None, :]).astype(jnp.bfloat16)
    partner_back = (partner_spots[:, None] == partner_key[None, :]).astype(jnp.bfloat16)

    first_source = (first_slot - owner + owners * clip_count) % owners
    entry_of = jnp.stack(
        [
            (first_source * depth + slots * block).reshape(times, per_device),
            (source * depth + (partner_slot % slots) * block).reshape(times, per_device),
        ],
        axis=1,
    ).reshape(-1)
    entry = (jnp.repeat(entry_of, block) + row_index % block)[:, None]
    entries = jnp.arange(owners * depth, dtype=jnp.int32)[None, :]
    rows = dot((entry == entries).astype(jnp.bfloat16), partners, ((1,), (0,)), jnp.bfloat16)
    rows = rows.reshape(times, 2 * per_device * block, feature)
    rows = lax.all_to_all(rows, both, 0, 0, axis_index_groups=home, tiled=True)

    my_ids = lax.dynamic_slice_in_dim(owned, place * per_device, per_device, 0)
    pair_lengths = jnp.take(lengths, my_ids.T)
    grads, losses = pair_call(rows.reshape(row_count, feature), pair_lengths, weight, block)

    grads = grads.reshape(times, 2 * per_device * block, feature)
    returned = lax.all_to_all(grads, both, 0, 0, axis_index_groups=home, tiled=True)
    returned = returned.reshape(row_count, feature)
    partner_sum = dot(partner_back, returned, ((1,), (0,))).astype(jnp.bfloat16)
    first_sum = dot(first_back, returned, ((1,), (0,))).astype(jnp.bfloat16)
    first_sum = with_scalars(first_sum, losses)
    first_sum = lax.ppermute(first_sum, both, back)
    partner_sum = partner_sum.reshape(owners, slots * block, feature)
    partner_sum = lax.all_to_all(partner_sum, both, 0, 0, axis_index_groups=plane, tiled=True)
    first_sum, losses = without_scalars(first_sum, per_device)
    partner_sum = lax.all_to_all(
        partner_sum, "tm", 0, 0, axis_index_groups=long_range, tiled=True
    )
    total = dot(spread_rows(chosen.T, block), partner_sum.reshape(-1, feature), ((1,), (0,)))
    total = (total + first_sum.astype(jnp.float32)).reshape(clip_count, block, feature)
    unit = as_float * scale
    gradient = scale * (total - unit * jnp.mean(total * unit, axis=-1, keepdims=True))
    return (losses, gradient.astype(jnp.bfloat16))


def solution(mesh):
    in_specs = (P("clip", "tm", None), P(), P(), P(("clip", "tm")))
    out_specs = (P(("clip", "tm")), P("clip", "tm", None))
    return jax.shard_map(shards, mesh=mesh, in_specs=in_specs, out_specs=out_specs, check_vma=False)
```

```python
import functools
import math

import jax
import jax.numpy as jnp
from jax import lax
from jax.experimental import pallas as pl
from jax.experimental.pallas import tpu as pltpu
from jax.sharding import PartitionSpec as P

score_scale = 2.0
spread_floor = 1.0
log_weight = 0.1
epsilon = 1e-06
slots = 4


def dot(left, right, contract, out=jnp.float32):
    return lax.dot_general(left, right, (contract, ((), ())), preferred_element_type=out)


def split(values, parts):
    pieces = []
    for _ in range(parts):
        piece = lax.reduce_precision(values, 8, 7)
        pieces.append(piece.astype(jnp.bfloat16))
        values = values - piece
    return pieces


def with_scalars(rows, scalars):
    pieces = jnp.stack(split(scalars, 3))
    pad = ((0, 8 - pieces.shape[0]), (0, rows.shape[1] - pieces.shape[1]))
    return jnp.concatenate([rows, jnp.pad(pieces, pad)], axis=0)


def without_scalars(packed, count):
    pieces = packed[-8:-5, :count].astype(jnp.float32)
    return packed[:-8], (pieces[0] + pieces[1]) + pieces[2]


def pair_math(n_first, n_partner, len_first, len_partner, weight, row_time, column_time):
    factor = score_scale / math.sqrt(n_first.shape[1])
    scores = dot(n_first, n_partner, ((1,), (1,))) * factor
    forward_exp = jnp.where(column_time < len_partner, jnp.exp(scores), 0.0)
    forward_prob = forward_exp * (1.0 / jnp.sum(forward_exp, axis=1, keepdims=True))
    prob = forward_prob.astype(jnp.bfloat16)
    high = scores.astype(jnp.bfloat16)
    low = (scores - high.astype(jnp.float32)).astype(jnp.bfloat16)
    backward_scores = dot(prob, high, ((1,), (1,))) + dot(prob, low, ((1,), (1,)))
    backward_exp = jnp.where(column_time < len_first, jnp.exp(backward_scores), 0.0)
    back_prob = backward_exp * (1.0 / jnp.sum(backward_exp, axis=1, keepdims=True))
    mean_time = jnp.sum(back_prob * column_time, axis=1, keepdims=True)
    offsets = column_time - mean_time
    squares = offsets * offsets
    variance = jnp.sum(back_prob * squares, axis=1, keepdims=True)
    spread = variance + spread_floor
    missed = row_time - mean_time
    ratio = missed / spread
    terms = missed * ratio + log_weight * jnp.log(spread)
    valid = row_time < len_first
    loss = jnp.sum(jnp.where(valid, terms, 0.0)) / len_first
    row_weight = jnp.where(valid, weight / len_first, 0.0)
    d_mean = -2.0 * ratio * row_weight
    d_spread = (log_weight / spread - ratio * ratio) * row_weight
    d_back = back_prob * (d_mean * offsets + d_spread * (squares - variance))
    d_low = d_back.astype(jnp.bfloat16)
    d_prob = dot(d_low, high, ((1,), (0,))) + dot(d_low, low, ((1,), (0,)))
    d_scores = forward_prob * (d_prob - jnp.sum(forward_prob * d_prob, axis=1, keepdims=True))
    d_scores = d_scores + dot(d_back.T.astype(jnp.bfloat16), prob, ((1,), (0,)))
    d_scores = d_scores * factor
    grad_first = dot(d_scores.astype(jnp.bfloat16), n_partner, ((1,), (0,)))
    grad_partner = dot(d_scores.T.astype(jnp.bfloat16), n_first, ((1,), (0,)))
    return loss, grad_first, grad_partner


def pair_kernel(block, weights, length_ref, weight_ref, rows_ref, out_ref, loss_ref, wide):
    total = rows_ref.shape[0]
    count = weights
    chunk = 2 * count * block
    sources = total // chunk
    frames = sources * block
    lanes = wide.shape[2]
    strips = wide.shape[0]
    for c in range(strips):
        wide[c] = rows_ref[:, c * lanes : (c + 1) * lanes].astype(jnp.float32)
    row = lax.broadcasted_iota(jnp.int32, (frames, 1), 0)
    row_time = ((row % sources) * block + row // sources).astype(jnp.float32)
    column = lax.broadcasted_iota(jnp.int32, (1, frames), 1)
    column_time = ((column % sources) * block + column // sources).astype(jnp.float32)

    def place(kind, pair, frame):
        return pl.ds((kind * count + pair) * block + frame, sources, stride=chunk)

    for pair in range(count):
        clips = [
            jnp.concatenate(
                [
                    jnp.concatenate(
                        [wide[c, place(kind, pair, f), :] for f in range(block)], axis=0
                    ).astype(jnp.bfloat16)
                    for c in range(strips)
                ],
                axis=1,
            )
            for kind in range(2)
        ]
        loss, *grads = pair_math(
            clips[0],
            clips[1],
            length_ref[0, pair].astype(jnp.float32),
            length_ref[1, pair].astype(jnp.float32),
            weight_ref[pair],
            row_time,
            column_time,
        )
        loss_ref[pair] = loss
        for kind in range(2):
            for f in range(block):
                part = grads[kind][f * sources : (f + 1) * sources]
                for c in range(strips):
                    wide[c, place(kind, pair, f), :] = part[:, c * lanes : (c + 1) * lanes]
    for c in range(strips):
        out_ref[:, c * lanes : (c + 1) * lanes] = wide[c].astype(jnp.bfloat16)


def pair_call(rows, lengths, weight, block):
    smem = pl.BlockSpec(memory_space=pltpu.SMEM)
    vmem = pl.BlockSpec(memory_space=pltpu.VMEM)
    return pl.pallas_call(
        functools.partial(pair_kernel, block, weight.shape[0]),
        out_shape=(
            jax.ShapeDtypeStruct(rows.shape, jnp.bfloat16),
            jax.ShapeDtypeStruct(weight.shape, jnp.float32),
        ),
        in_specs=[smem, smem, vmem],
        out_specs=(vmem, smem),
        scratch_shapes=[pltpu.VMEM((rows.shape[1] // 128, rows.shape[0], 128), jnp.float32)],
        compiler_params=pltpu.CompilerParams(vmem_limit_bytes=40 * 1024 * 1024),
    )(lengths, weight, rows)


def inverse_norm(rows):
    as_float = rows.astype(jnp.float32)
    return lax.rsqrt(jnp.mean(as_float * as_float, axis=-1, keepdims=True) + epsilon)


def spread_rows(hot, block):
    rows = jnp.arange(hot.shape[0] * block, dtype=jnp.int32)
    columns = jnp.arange(hot.shape[1] * block, dtype=jnp.int32)
    same = rows[:, None] % block == columns[None, :] % block
    wide = jnp.repeat(jnp.repeat(hot, block, axis=0), block, axis=1)
    return jnp.where(same, wide, 0).astype(jnp.bfloat16)


def shards(embeddings, lengths, pairs, scaled_weight):
    owners = lax.axis_size("clip")
    times = lax.axis_size("tm")
    clip_count, block, feature = embeddings.shape
    per_device = scaled_weight.shape[0]
    per_owner = per_device * times
    row_width = block * feature
    spots = times // owners
    column = lax.axis_index("clip")
    time_index = lax.axis_index("tm")
    owner = time_index // spots
    spot = time_index % spots
    turn = (column - owner + owners) % owners
    place = turn * spots + spot

    long_range = [[a + spots * i for i in range(owners)] for a in range(spots)]
    home = [
        [((m + c) % owners) * times + spots * c + q for m in range(owners) for q in range(spots)]
        for c in range(owners)
    ]
    plane = [
        [((m + t // spots) % owners) * times + t for m in range(owners)] for t in range(times)
    ]
    swap = [
        (c * times + t, ((t // spots + c) % owners) * times + c * spots + t % spots)
        for c in range(owners)
        for t in range(times)
    ]
    back = [(there, here) for here, there in swap]
    both = ("clip", "tm")

    lanes = 128
    pieces = jnp.pad(jnp.stack(split(scaled_weight, 3)).reshape(-1), (0, lanes - 3 * per_device))
    tail = jnp.broadcast_to(pieces, (clip_count, block, lanes))
    spread = jnp.concatenate([embeddings, tail], axis=2)
    spread = lax.all_to_all(spread, "clip", 0, 0, tiled=True)
    weight_rows = spread[:, 0, feature:]
    spread = spread[:, :, :feature].reshape(clip_count * block, feature)
    spread = (spread.astype(jnp.float32) * inverse_norm(spread)).astype(jnp.bfloat16)
    flat = embeddings.reshape(clip_count * block, feature)
    scale = inverse_norm(flat)
    unit = flat.astype(jnp.float32) * scale
    normalized = unit.astype(jnp.bfloat16)

    grouped = pairs.reshape(owners, per_owner, 2)
    clips = jnp.arange(owners * clip_count, dtype=jnp.int32)
    used = jnp.any(grouped[:, :, 1, None] == clips[None, None, :], axis=1)
    before = (clips[:, None] // clip_count == clips[None, :] // clip_count) & (
        clips[:, None] < clips[None, :]
    )
    rank = dot(used.astype(jnp.bfloat16), before.astype(jnp.bfloat16), ((1,), (0,)))
    rank = jnp.where(used, rank.astype(jnp.int32), -1)
    mine = lax.dynamic_slice_in_dim(rank, column * clip_count, clip_count, 1)
    slot_ids = jnp.arange(slots, dtype=jnp.int32)
    chosen = mine[:, None, :] == slot_ids[None, :, None]
    chosen = chosen.reshape(owners * slots, clip_count).astype(jnp.bfloat16)

    depth = (slots + 1) * block
    parts = 3
    width = feature // parts
    chunk = -(-parts * depth // 16) * 16
    own = jnp.where(jnp.eye(owners, dtype=bool), slots, -1)
    wanted = jnp.concatenate([mine, own], axis=1).astype(jnp.bfloat16)
    out_row = jnp.arange(owners * chunk, dtype=jnp.int32)
    in_row = jnp.arange(2 * clip_count * block, dtype=jnp.int32)
    of_owner = out_row[:, None] // chunk == jnp.arange(owners, dtype=jnp.int32)[None, :]
    of_source = jnp.arange(2 * clip_count, dtype=jnp.int32)[:, None] == in_row[None, :] // block
    wanted = dot(of_owner.astype(jnp.bfloat16), wanted, ((1,), (0,)), jnp.bfloat16)
    wanted = dot(wanted, of_source.astype(jnp.bfloat16), ((1,), (0,))).astype(jnp.int32)
    out_part = (out_row % chunk // depth)[:, None]
    out_depth = (out_row % chunk % depth)[:, None]
    picked = (wanted == out_depth // block) & (out_depth % block == in_row[None, :] % block)
    pick = [picked & (out_part == h) for h in range(parts)]
    pick.append(of_owner & (out_part == parts) & (out_depth == 0))
    pick = jnp.concatenate(pick, axis=1).astype(jnp.bfloat16)
    sources = jnp.concatenate([normalized, spread], axis=0)
    sources = [sources[:, h * width : (h + 1) * width] for h in range(parts)]
    sources.append(jnp.pad(weight_rows, ((0, 0), (0, width - lanes))))
    outgoing = dot(pick, jnp.concatenate(sources, axis=0), ((1,), (0,)), jnp.bfloat16)
    outgoing = outgoing.reshape(owners, chunk, width)
    outgoing = lax.all_to_all(
        outgoing, "tm", 0, 0, axis_index_groups=long_range, tiled=True
    )
    partners = lax.all_to_all(outgoing, both, 0, 0, axis_index_groups=plane, tiled=True)
    pieces = partners[0, parts * depth, : 3 * per_device].astype(jnp.float32)
    pieces = pieces.reshape(3, per_device)
    weight = (pieces[0] + pieces[1]) + pieces[2]
    partners = jnp.concatenate(
        [partners[:, h * depth : (h + 1) * depth] for h in range(parts)], axis=2
    ).reshape(owners * depth, feature)

    owned = lax.dynamic_index_in_dim(grouped, owner, 0, keepdims=False)
    owned_rank = lax.dynamic_index_in_dim(rank, owner, 0, keepdims=False)
    first_slot = owned[:, 0] - owner * clip_count
    partner_is = owned[:, 1][:, None] == clips[None, :]
    partner_slot = jnp.sum(jnp.where(partner_is, owned_rank[None, :], 0), axis=1)
    source = (owned[:, 1] // clip_count - owner + owners) % owners
    partner_slot = partner_slot + source * slots
    slot_of = jnp.stack(
        [first_slot.reshape(times, per_device), partner_slot.reshape(times, per_device)], axis=1
    ).reshape(-1)
    row_count = 2 * per_owner * block
    row_slot = jnp.repeat(slot_of, block)
    row_index = jnp.arange(row_count, dtype=jnp.int32)
    row_key = row_slot * block + row_index % block
    is_first = (row_index // (per_device * block)) % 2 == 0
    first_key = jnp.where(is_first, row_key, -1)
    partner_key = jnp.where(is_first, -1, row_key)
    first_spots = jnp.arange(clip_count * block, dtype=jnp.int32)
    partner_spots = jnp.arange(owners * slots * block, dtype=jnp.int32)
    first_back = (first_spots[:, None] == first_key[None, :]).astype(jnp.bfloat16)
    partner_back = (partner_spots[:, None] == partner_key[None, :]).astype(jnp.bfloat16)

    first_source = (first_slot - owner + owners * clip_count) % owners
    entry_of = jnp.stack(
        [
            (first_source * depth + slots * block).reshape(times, per_device),
            (source * depth + (partner_slot % slots) * block).reshape(times, per_device),
        ],
        axis=1,
    ).reshape(-1)
    entry = (jnp.repeat(entry_of, block) + row_index % block)[:, None]
    entries = jnp.arange(owners * depth, dtype=jnp.int32)[None, :]
    entry_hot = lax.optimization_barrier((entry == entries).astype(jnp.bfloat16))
    rows = dot(entry_hot, partners, ((1,), (0,)), jnp.bfloat16)
    rows = rows.reshape(times, 2 * per_device * block, feature)
    rows = lax.all_to_all(rows, both, 0, 0, axis_index_groups=home, tiled=True)

    my_ids = lax.dynamic_slice_in_dim(owned, place * per_device, per_device, 0)
    pair_lengths = jnp.take(lengths, my_ids.T)
    grads, losses = pair_call(rows.reshape(row_count, feature), pair_lengths, weight, block)

    grads = grads.reshape(times, 2 * per_device * block, feature)
    returned = lax.all_to_all(grads, both, 0, 0, axis_index_groups=home, tiled=True)
    returned = returned.reshape(row_count, feature)
    partner_sum = dot(partner_back, returned, ((1,), (0,))).astype(jnp.bfloat16)
    first_sum = dot(first_back, returned, ((1,), (0,))).astype(jnp.bfloat16)
    first_sum = with_scalars(first_sum, losses)
    first_sum = lax.ppermute(first_sum, both, back)
    partner_sum = partner_sum.reshape(owners, slots * block, feature)
    partner_sum = lax.all_to_all(partner_sum, both, 0, 0, axis_index_groups=plane, tiled=True)
    first_sum, losses = without_scalars(first_sum, per_device)
    partner_sum = lax.all_to_all(
        partner_sum, "tm", 0, 0, axis_index_groups=long_range, tiled=True
    )
    total = dot(spread_rows(chosen.T, block), partner_sum.reshape(-1, feature), ((1,), (0,)))
    total = total + first_sum.astype(jnp.float32)
    gradient = scale * (total - unit * jnp.mean(total * unit, axis=-1, keepdims=True))
    gradient = gradient.reshape(clip_count, block, feature)
    return (losses, gradient.astype(jnp.bfloat16))


def solution(mesh):
    in_specs = (P("clip", "tm", None), P(), P(), P(("clip", "tm")))
    out_specs = (P(("clip", "tm")), P("clip", "tm", None))
    return jax.shard_map(shards, mesh=mesh, in_specs=in_specs, out_specs=out_specs, check_vma=False)
```

```python
import functools
import math

import jax
import jax.numpy as jnp
from jax import lax
from jax.experimental import pallas as pl
from jax.experimental.pallas import tpu as pltpu
from jax.sharding import PartitionSpec as P

score_scale = 2.0
spread_floor = 1.0
log_weight = 0.1
epsilon = 1e-06
slots = 4


def dot(left, right, contract, out=jnp.float32):
    return lax.dot_general(left, right, (contract, ((), ())), preferred_element_type=out)


def split(values, parts):
    pieces = []
    for _ in range(parts):
        piece = lax.reduce_precision(values, 8, 7)
        pieces.append(piece.astype(jnp.bfloat16))
        values = values - piece
    return pieces


def with_scalars(rows, scalars):
    pieces = jnp.stack(split(scalars, 3))
    pad = ((0, 8 - pieces.shape[0]), (0, rows.shape[1] - pieces.shape[1]))
    return jnp.concatenate([rows, jnp.pad(pieces, pad)], axis=0)


def without_scalars(packed, count):
    pieces = packed[-8:-5, :count].astype(jnp.float32)
    return packed[:-8], (pieces[0] + pieces[1]) + pieces[2]


def pair_math(n_first, n_partner, len_first, len_partner, weight, row_time, column_time):
    factor = score_scale / math.sqrt(n_first.shape[1])
    scores = dot(n_first, n_partner, ((1,), (1,))) * factor
    forward_exp = jnp.where(column_time < len_partner, jnp.exp(scores), 0.0)
    forward_prob = forward_exp * (1.0 / jnp.sum(forward_exp, axis=1, keepdims=True))
    prob = forward_prob.astype(jnp.bfloat16)
    high = scores.astype(jnp.bfloat16)
    low = (scores - high.astype(jnp.float32)).astype(jnp.bfloat16)
    backward_scores = dot(prob, high, ((1,), (1,))) + dot(prob, low, ((1,), (1,)))
    backward_exp = jnp.where(column_time < len_first, jnp.exp(backward_scores), 0.0)
    back_prob = backward_exp * (1.0 / jnp.sum(backward_exp, axis=1, keepdims=True))
    mean_time = jnp.sum(back_prob * column_time, axis=1, keepdims=True)
    offsets = column_time - mean_time
    squares = offsets * offsets
    variance = jnp.sum(back_prob * squares, axis=1, keepdims=True)
    spread = variance + spread_floor
    missed = row_time - mean_time
    ratio = missed / spread
    terms = missed * ratio + log_weight * jnp.log(spread)
    valid = row_time < len_first
    loss = jnp.sum(jnp.where(valid, terms, 0.0)) / len_first
    row_weight = jnp.where(valid, weight / len_first, 0.0)
    d_mean = -2.0 * ratio * row_weight
    d_spread = (log_weight / spread - ratio * ratio) * row_weight
    d_back = back_prob * (d_mean * offsets + d_spread * (squares - variance))
    d_low = d_back.astype(jnp.bfloat16)
    d_prob = dot(d_low, high, ((1,), (0,))) + dot(d_low, low, ((1,), (0,)))
    d_scores = forward_prob * (d_prob - jnp.sum(forward_prob * d_prob, axis=1, keepdims=True))
    d_scores = d_scores + dot(d_back.T.astype(jnp.bfloat16), prob, ((1,), (0,)))
    d_scores = d_scores * factor
    grad_first = dot(d_scores.astype(jnp.bfloat16), n_partner, ((1,), (0,)))
    grad_partner = dot(d_scores.T.astype(jnp.bfloat16), n_first, ((1,), (0,)))
    return loss, grad_first, grad_partner


def pair_kernel(block, weights, length_ref, weight_ref, rows_ref, out_ref, loss_ref, wide):
    total = rows_ref.shape[0]
    count = weights
    chunk = 2 * count * block
    sources = total // chunk
    frames = sources * block
    pitch = chunk + 1
    lanes = wide.shape[2]
    strips = wide.shape[0]
    for c in range(strips):
        strip = rows_ref[:, c * lanes : (c + 1) * lanes].astype(jnp.float32)
        for d in range(sources):
            wide[c, d * pitch : d * pitch + chunk] = strip[d * chunk : (d + 1) * chunk]
    row = lax.broadcasted_iota(jnp.int32, (frames, 1), 0)
    row_time = ((row % sources) * block + row // sources).astype(jnp.float32)
    column = lax.broadcasted_iota(jnp.int32, (1, frames), 1)
    column_time = ((column % sources) * block + column // sources).astype(jnp.float32)

    def place(kind, pair, frame):
        return pl.ds((kind * count + pair) * block + frame, sources, stride=pitch)

    for pair in range(count):
        clips = [
            jnp.concatenate(
                [
                    jnp.concatenate(
                        [wide[c, place(kind, pair, f), :] for f in range(block)], axis=0
                    ).astype(jnp.bfloat16)
                    for c in range(strips)
                ],
                axis=1,
            )
            for kind in range(2)
        ]
        loss, *grads = pair_math(
            clips[0],
            clips[1],
            length_ref[0, pair].astype(jnp.float32),
            length_ref[1, pair].astype(jnp.float32),
            weight_ref[pair],
            row_time,
            column_time,
        )
        loss_ref[pair] = loss
        for kind in range(2):
            for f in range(block):
                part = grads[kind][f * sources : (f + 1) * sources]
                for c in range(strips):
                    wide[c, place(kind, pair, f), :] = part[:, c * lanes : (c + 1) * lanes]
    for c in range(strips):
        for d in range(sources):
            part = wide[c, d * pitch : d * pitch + chunk]
            out_ref[d * chunk : (d + 1) * chunk, c * lanes : (c + 1) * lanes] = part.astype(
                jnp.bfloat16
            )


def pair_call(rows, lengths, weight, block):
    padded = rows.shape[0] + rows.shape[0] // (2 * weight.shape[0] * block)
    smem = pl.BlockSpec(memory_space=pltpu.SMEM)
    vmem = pl.BlockSpec(memory_space=pltpu.VMEM)
    return pl.pallas_call(
        functools.partial(pair_kernel, block, weight.shape[0]),
        out_shape=(
            jax.ShapeDtypeStruct(rows.shape, jnp.bfloat16),
            jax.ShapeDtypeStruct(weight.shape, jnp.float32),
        ),
        in_specs=[smem, smem, vmem],
        out_specs=(vmem, smem),
        scratch_shapes=[pltpu.VMEM((rows.shape[1] // 128, padded, 128), jnp.float32)],
        compiler_params=pltpu.CompilerParams(vmem_limit_bytes=40 * 1024 * 1024),
    )(lengths, weight, rows)


def inverse_norm(rows):
    as_float = rows.astype(jnp.float32)
    return lax.rsqrt(jnp.mean(as_float * as_float, axis=-1, keepdims=True) + epsilon)


def spread_rows(hot, block):
    rows = jnp.arange(hot.shape[0] * block, dtype=jnp.int32)
    columns = jnp.arange(hot.shape[1] * block, dtype=jnp.int32)
    same = rows[:, None] % block == columns[None, :] % block
    wide = jnp.repeat(jnp.repeat(hot, block, axis=0), block, axis=1)
    return jnp.where(same, wide, 0).astype(jnp.bfloat16)


def shards(embeddings, lengths, pairs, scaled_weight):
    owners = lax.axis_size("clip")
    times = lax.axis_size("tm")
    clip_count, block, feature = embeddings.shape
    per_device = scaled_weight.shape[0]
    per_owner = per_device * times
    row_width = block * feature
    spots = times // owners
    column = lax.axis_index("clip")
    time_index = lax.axis_index("tm")
    owner = time_index // spots
    spot = time_index % spots
    turn = (column - owner + owners) % owners
    place = turn * spots + spot

    long_range = [[a + spots * i for i in range(owners)] for a in range(spots)]
    home = [
        [((m + c) % owners) * times + spots * c + q for m in range(owners) for q in range(spots)]
        for c in range(owners)
    ]
    plane = [
        [((m + t // spots) % owners) * times + t for m in range(owners)] for t in range(times)
    ]
    swap = [
        (c * times + t, ((t // spots + c) % owners) * times + c * spots + t % spots)
        for c in range(owners)
        for t in range(times)
    ]
    back = [(there, here) for here, there in swap]
    both = ("clip", "tm")

    lanes = 128
    pieces = jnp.pad(jnp.stack(split(scaled_weight, 3)).reshape(-1), (0, lanes - 3 * per_device))
    tail = jnp.broadcast_to(pieces, (clip_count, block, lanes))
    spread = jnp.concatenate([embeddings, tail], axis=2)
    spread = lax.all_to_all(spread, "clip", 0, 0, tiled=True)
    weight_rows = spread[:, 0, feature:]
    spread = spread[:, :, :feature].reshape(clip_count * block, feature)
    spread = (spread.astype(jnp.float32) * inverse_norm(spread)).astype(jnp.bfloat16)
    flat = embeddings.reshape(clip_count * block, feature)
    scale = inverse_norm(flat)
    unit = flat.astype(jnp.float32) * scale
    normalized = unit.astype(jnp.bfloat16)

    grouped = pairs.reshape(owners, per_owner, 2)
    clips = jnp.arange(owners * clip_count, dtype=jnp.int32)
    used = jnp.any(grouped[:, :, 1, None] == clips[None, None, :], axis=1)
    before = (clips[:, None] // clip_count == clips[None, :] // clip_count) & (
        clips[:, None] < clips[None, :]
    )
    rank = dot(used.astype(jnp.bfloat16), before.astype(jnp.bfloat16), ((1,), (0,)))
    rank = jnp.where(used, rank.astype(jnp.int32), -1)
    mine = lax.dynamic_slice_in_dim(rank, column * clip_count, clip_count, 1)
    slot_ids = jnp.arange(slots, dtype=jnp.int32)
    chosen = mine[:, None, :] == slot_ids[None, :, None]
    chosen = chosen.reshape(owners * slots, clip_count).astype(jnp.bfloat16)

    depth = (slots + 1) * block
    parts = 3
    width = feature // parts
    chunk = -(-parts * depth // 16) * 16
    own = jnp.where(jnp.eye(owners, dtype=bool), slots, -1)
    wanted = jnp.concatenate([mine, own], axis=1).astype(jnp.bfloat16)
    out_row = jnp.arange(owners * chunk, dtype=jnp.int32)
    in_row = jnp.arange(2 * clip_count * block, dtype=jnp.int32)
    of_owner = out_row[:, None] // chunk == jnp.arange(owners, dtype=jnp.int32)[None, :]
    of_source = jnp.arange(2 * clip_count, dtype=jnp.int32)[:, None] == in_row[None, :] // block
    wanted = dot(of_owner.astype(jnp.bfloat16), wanted, ((1,), (0,)), jnp.bfloat16)
    wanted = dot(wanted, of_source.astype(jnp.bfloat16), ((1,), (0,))).astype(jnp.int32)
    out_part = (out_row % chunk // depth)[:, None]
    out_depth = (out_row % chunk % depth)[:, None]
    picked = (wanted == out_depth // block) & (out_depth % block == in_row[None, :] % block)
    pick = [picked & (out_part == h) for h in range(parts)]
    pick.append(of_owner & (out_part == parts) & (out_depth == 0))
    pick = jnp.concatenate(pick, axis=1).astype(jnp.bfloat16)
    sources = jnp.concatenate([normalized, spread], axis=0)
    sources = [sources[:, h * width : (h + 1) * width] for h in range(parts)]
    sources.append(jnp.pad(weight_rows, ((0, 0), (0, width - lanes))))
    outgoing = dot(pick, jnp.concatenate(sources, axis=0), ((1,), (0,)), jnp.bfloat16)
    outgoing = outgoing.reshape(owners, chunk, width)
    outgoing = lax.all_to_all(
        outgoing, "tm", 0, 0, axis_index_groups=long_range, tiled=True
    )
    partners = lax.all_to_all(outgoing, both, 0, 0, axis_index_groups=plane, tiled=True)
    pieces = partners[0, parts * depth, : 3 * per_device].astype(jnp.float32)
    pieces = pieces.reshape(3, per_device)
    weight = (pieces[0] + pieces[1]) + pieces[2]
    partners = jnp.concatenate(
        [partners[:, h * depth : (h + 1) * depth] for h in range(parts)], axis=2
    ).reshape(owners * depth, feature)

    owned = lax.dynamic_index_in_dim(grouped, owner, 0, keepdims=False)
    owned_rank = lax.dynamic_index_in_dim(rank, owner, 0, keepdims=False)
    first_slot = owned[:, 0] - owner * clip_count
    partner_is = owned[:, 1][:, None] == clips[None, :]
    partner_slot = jnp.sum(jnp.where(partner_is, owned_rank[None, :], 0), axis=1)
    source = (owned[:, 1] // clip_count - owner + owners) % owners
    partner_slot = partner_slot + source * slots
    slot_of = jnp.stack(
        [first_slot.reshape(times, per_device), partner_slot.reshape(times, per_device)], axis=1
    ).reshape(-1)
    row_count = 2 * per_owner * block
    row_slot = jnp.repeat(slot_of, block)
    row_index = jnp.arange(row_count, dtype=jnp.int32)
    row_key = row_slot * block + row_index % block
    is_first = (row_index // (per_device * block)) % 2 == 0
    first_key = jnp.where(is_first, row_key, -1)
    partner_key = jnp.where(is_first, -1, row_key)
    first_spots = jnp.arange(clip_count * block, dtype=jnp.int32)
    partner_spots = jnp.arange(owners * slots * block, dtype=jnp.int32)
    first_back = (first_spots[:, None] == first_key[None, :]).astype(jnp.bfloat16)
    partner_back = (partner_spots[:, None] == partner_key[None, :]).astype(jnp.bfloat16)

    first_source = (first_slot - owner + owners * clip_count) % owners
    entry_of = jnp.stack(
        [
            (first_source * depth + slots * block).reshape(times, per_device),
            (source * depth + (partner_slot % slots) * block).reshape(times, per_device),
        ],
        axis=1,
    ).reshape(-1)
    entry = (jnp.repeat(entry_of, block) + row_index % block)[:, None]
    entries = jnp.arange(owners * depth, dtype=jnp.int32)[None, :]
    entry_hot = lax.optimization_barrier((entry == entries).astype(jnp.bfloat16))
    rows = dot(entry_hot, partners, ((1,), (0,)), jnp.bfloat16)
    rows = rows.reshape(times, 2 * per_device * block, feature)
    rows = lax.all_to_all(rows, both, 0, 0, axis_index_groups=home, tiled=True)

    my_ids = lax.dynamic_slice_in_dim(owned, place * per_device, per_device, 0)
    pair_lengths = jnp.take(lengths, my_ids.T)
    grads, losses = pair_call(rows.reshape(row_count, feature), pair_lengths, weight, block)

    grads = grads.reshape(times, 2 * per_device * block, feature)
    returned = lax.all_to_all(grads, both, 0, 0, axis_index_groups=home, tiled=True)
    returned = returned.reshape(row_count, feature)
    partner_sum = dot(partner_back, returned, ((1,), (0,))).astype(jnp.bfloat16)
    first_sum = dot(first_back, returned, ((1,), (0,))).astype(jnp.bfloat16)
    first_sum = with_scalars(first_sum, losses)
    first_sum = lax.ppermute(first_sum, both, back)
    partner_sum = partner_sum.reshape(owners, slots * block, feature)
    partner_sum = lax.all_to_all(partner_sum, both, 0, 0, axis_index_groups=plane, tiled=True)
    first_sum, losses = without_scalars(first_sum, per_device)
    partner_sum = lax.all_to_all(
        partner_sum, "tm", 0, 0, axis_index_groups=long_range, tiled=True
    )
    total = dot(spread_rows(chosen.T, block), partner_sum.reshape(-1, feature), ((1,), (0,)))
    total = total + first_sum.astype(jnp.float32)
    gradient = scale * (total - unit * jnp.mean(total * unit, axis=-1, keepdims=True))
    gradient = gradient.reshape(clip_count, block, feature)
    return (losses, gradient.astype(jnp.bfloat16))


def solution(mesh):
    in_specs = (P("clip", "tm", None), P(), P(), P(("clip", "tm")))
    out_specs = (P(("clip", "tm")), P("clip", "tm", None))
    return jax.shard_map(shards, mesh=mesh, in_specs=in_specs, out_specs=out_specs, check_vma=False)
```
